128 devices in a mesh: tensor: 4 (over z), island: 8 (over y, core), region: 4 (over x).
Axes of the slice: x: 4, y: 4, z: 4, core: 2. Of those that a mesh axis runs over, the one named last changes fastest.
Arguments:
- global_params: float32 [512, 16384], P(None, 'tensor'), may hold values from -6 to 6
- local_params: bfloat16 [4, 8, 512, 16384], P('region', 'island', None, 'tensor'), may hold values from -6 to 6
- error_buf: float32 [4, 8, 512, 16384], P('region', 'island', None, 'tensor'), may hold values from -6 to 6
- momentum: float32 [512, 16384], P(('island', 'region'), 'tensor'), may hold values from -6 to 6
- kept: int32 [4, 8, 4, 16], P('region', 'island', 'tensor'), may hold values from 0 to 127, as said below
- counts: int32 [4, 8, 4], P('region', 'island', 'tensor'), may hold values from 1 to 16
Outputs:
- new_params: float32 [512, 16384], P(None, 'tensor')
- new_error: float32 [4, 8, 512, 16384], P('region', 'island', None, 'tensor')
- new_momentum: float32 [512, 16384], P(('island', 'region'), 'tensor')
The draws below stay inside these ranges and needn't reach their ends.
Inputs may be any that keep to these rules, and one draw needn't show every extreme that they name: The first counts[r, i, t] entries of kept[r, i, t] are distinct block numbers; the list of one device is at most 16 long and some device's list is exactly 16 long.
All inputs are finite; a program needn't handle non-finite values.
Results may differ from the reference program's by a relative error of at most 0.00085.
Values may be sent and summed in bfloat16 or wider, within the bound.
No kernel may reach another device: no remote copies, remote signals or barrier semaphores. Data moves between devices by JAX's collectives and lax.ppermute only.
A program may use at most 128 MiB of HBM per device.

```python
import jax
import jax.numpy as jnp
from jax import lax

D = 16384
ROWS = 512
BLOCK = 128
KMAX = 16
REGIONS = 4
ISLANDS = 8
SHARDS = 4
BLOCKS_DEV = 128


def draw_kept(key, part):
    key = jax.random.fold_in(key, 11)
    total = REGIONS * ISLANDS * SHARDS
    keys = jax.random.split(key, total)
    orders = jax.vmap(lambda k: jax.random.permutation(k, BLOCKS_DEV))(keys)[:, :KMAX]
    return orders.reshape(REGIONS, ISLANDS, SHARDS, KMAX).astype(jnp.int32)


def draw_counts(key, part):
    key = jax.random.fold_in(key, 12)
    first, second = jax.random.split(key)
    total = REGIONS * ISLANDS * SHARDS
    values = jax.random.randint(first, (total,), 1, KMAX // 2 + 1)
    chosen = jax.random.randint(second, (), 0, total)
    values = jnp.where(jnp.arange(total) == chosen, KMAX, values)
    return values.reshape(REGIONS, ISLANDS, SHARDS).astype(jnp.int32)


def steps_of(stream_key, dims, pieces, low, high):
    def one(dim, blocks):
        steps = jax.random.uniform(jax.random.fold_in(jax.random.fold_in(stream_key, 6), dim), (blocks,), jnp.float32, low / len(pieces), high / len(pieces))
        return jnp.repeat(jnp.exp(steps), dims[dim] // blocks).reshape((-1,) + (1,) * (len(dims) - dim - 1))

    factor_of = one(*pieces[0])
    for cut in pieces[1:]:
        factor_of = factor_of * one(*cut)
    return factor_of


def scatter_about(key, extent, deviation, bound, shards=(), kind=jnp.bfloat16):
    factor_of = steps_of(key, extent, shards, -0.22, 0.18) if shards else 1.0
    drawn = jax.random.normal(key, extent, jnp.float32) * deviation * factor_of
    return jnp.minimum(jnp.maximum(drawn, -bound), bound).astype(kind)


def setup_inputs(seed: int = 0) -> dict:
    key_of = jax.random.split(jax.random.key(seed), 7)
    global_params = scatter_about(key_of[0], (ROWS, D), 1.0, 6.0, ((1, 4),), jnp.float32)
    local_params = scatter_about(key_of[1], (REGIONS, ISLANDS, ROWS, D), 1.0, 6.0, ((0, 4), (1, 8), (3, 4)))
    error_buf = scatter_about(key_of[2], (REGIONS, ISLANDS, ROWS, D), 1.0, 6.0, ((0, 4), (1, 8), (3, 4)), jnp.float32)
    momentum = scatter_about(key_of[3], (ROWS, D), 1.0, 6.0, ((0, 32), (1, 4)), jnp.float32)
    kept = draw_kept(jax.random.fold_in(key_of[6], 71), 0)
    counts = draw_counts(jax.random.fold_in(key_of[6], 71), 0)
    return {"global_params": global_params, "local_params": local_params, "error_buf": error_buf, "momentum": momentum, "kept": kept, "counts": counts}


def reference(global_params, local_params, error_buf, momentum, kept, counts):
    col_blocks = D // (BLOCK * SHARDS)
    row_blocks = ROWS // BLOCK
    acc = 0.95 * error_buf + (global_params[None, None] - local_params.astype(jnp.float32))
    live = jnp.arange(KMAX, dtype=jnp.int32)[None, None, None, :] < counts[..., None]
    onehot = (kept[..., None] == jnp.arange(BLOCKS_DEV, dtype=jnp.int32)) & live[..., None]
    chosen = jnp.any(onehot, axis=3)
    chosen = chosen.reshape(REGIONS, ISLANDS, SHARDS, row_blocks, col_blocks)
    chosen = jnp.transpose(chosen, (0, 1, 3, 2, 4)).reshape(REGIONS, ISLANDS, row_blocks, SHARDS * col_blocks)
    chosen = jnp.repeat(jnp.repeat(chosen, BLOCK, axis=2), BLOCK, axis=3)
    rounded = lax.optimization_barrier(acc.astype(jnp.bfloat16)).astype(jnp.float32)
    message = jnp.where(chosen, rounded, jnp.float32(0.0))
    new_error = acc - message
    average = jnp.sum(message, axis=(0, 1)) / (REGIONS * ISLANDS)
    new_momentum = 0.9 * momentum + average
    new_params = global_params - 0.7 * (average + 0.9 * new_momentum)
    return new_params, new_error, new_momentum
```

```python
import functools

import jax
import jax.numpy as jnp
from jax import lax
from jax.experimental import pallas as pl
from jax.experimental.pallas import tpu as pltpu
from jax.sharding import PartitionSpec as P

BLOCK = 128
PARTS = 4
DEVICES = 32
EXTRA = 16
AXES = ("island", "region")
SCALE = 2.0**24
MIB = 2**20
F32 = jnp.float32
BF16 = jnp.bfloat16


def place():
    island = lax.axis_index("island")
    return island // 2, island % 2, lax.axis_index("region")


def move(array, step):
    pairs = []
    for p in range(DEVICES):
        y, c, x = p // 8, p // 4 % 2, p % 4
        y, c, x = step(y, c, x)
        pairs.append((p, 8 * (y % 4) + 4 * (c % 2) + x % 4))
    return lax.ppermute(array, AXES, pairs)


def encode(v):
    v = v * SCALE
    s = v * v
    return jnp.where(v < 0, -(s * s), s * s).astype(BF16)


def decode(code):
    w = code.astype(F32)
    v = lax.rsqrt(lax.rsqrt(jnp.abs(w))) * (1.0 / SCALE)
    return jnp.where(w < 0, -v, v)


def pick(index, choices):
    out = choices[-1]
    for i in range(len(choices) - 2, -1, -1):
        out = jnp.where(index == i, choices[i], out)
    return out


def pack_kernel(ids, count, pos, g, l, e, mom, pay, m0, m1, m2, m3, gb, lb, eb, sems):
    y, x = pos[0], pos[2]
    slots = gb.shape[0]
    copies = []
    for k in range(slots):
        rows = pl.ds(pl.multiple_of(ids[k] // 32 * BLOCK, BLOCK), BLOCK)
        cols = pl.ds(pl.multiple_of(ids[k] % 32 * BLOCK, BLOCK), BLOCK)
        copies.append([
            pltpu.make_async_copy(src.at[rows, cols], dst.at[k], sems.at[i, k])
            for i, (src, dst) in enumerate(((g, gb), (l, lb), (e, eb)))
        ])
        for copy in copies[-1]:
            copy.start()
    for d, out in enumerate((m0, m1, m2, m3)):
        out[...] = pick((y + d) % 4, [mom[4 * q : 4 * q + 4, :] for q in range(4)])
    lane = lax.broadcasted_iota(jnp.int32, (EXTRA, BLOCK), 1)
    vec = jnp.zeros((EXTRA, BLOCK), F32)
    for k in range(slots):
        vec = jnp.where(lane % 64 // 4 == k, ids[k].astype(F32), vec)
    vec = jnp.where(lane // 64 == x % 2, vec, 0.0).astype(BF16)
    for p in range(DEVICES):
        pay[p, 64 : 64 + EXTRA, :] = vec
    for group in range(slots // 4):
        for k in range(4 * group, 4 * group + 4):
            for copy in copies[k]:
                copy.wait()
        for r in range(8):
            rows = slice(16 * r, 16 * r + 16)
            tiles = []
            for k in range(4 * group, 4 * group + 4):
                acc = 0.95 * eb[k, rows, :] + (gb[k, rows, :] - lb[k, rows, :].astype(F32))
                tiles.append(jnp.where(k < count[0], acc, 0.0))
            for q in range(4):
                tile = jnp.concatenate([t[4 * q : 4 * q + 4] for t in tiles], axis=0)
                pay[8 * q + r, 16 * group : 16 * group + 16, :] = tile.astype(BF16)


def share_kernel(pos, recv, g, m0, m1, m2, m3, code, n0, n1, n2, n3, gb, mb, nb, sems):
    y, c, x = pos[0], pos[1], pos[2]
    r = 4 * c + x
    copies = []
    for q in range(4):
        rows = pl.ds(pl.multiple_of(q * BLOCK + 16 * r, 16), 16)
        copies.append(pltpu.make_async_copy(g.at[rows, :], gb.at[q], sems.at[q]))
        copies[-1].start()
    for d, m in enumerate((m0, m1, m2, m3)):
        mb[d] = m[...]
    row = lax.broadcasted_iota(jnp.int32, (512, BLOCK), 0)
    lane = lax.broadcasted_iota(jnp.int32, (512, BLOCK), 1)
    want = (row // 4 % 4 * 32 + row // 16) * 4 + row % 4
    want = (want - lane % 4).astype(F32)
    total = jnp.zeros((512, BLOCK), F32)
    for i in range(0, DEVICES, 4):
        halves = []
        for h in (i, i + 2):
            pair = recv[h, 64 : 64 + EXTRA, :].astype(F32) + recv[h + 1, 64 : 64 + EXTRA, :].astype(F32)
            halves.append((want == 4.0 * pair[0:1, :]).astype(F32).astype(BF16))
        table = jnp.concatenate(halves, axis=1)
        values = jnp.concatenate([recv[i + s, 0:64, :] for s in range(4)], axis=0)
        total = total + jnp.dot(table, values, preferred_element_type=F32)
    for copy in copies:
        copy.wait()
    for b in range(32):
        cols = slice(BLOCK * b, BLOCK * b + BLOCK)
        average = total[16 * b : 16 * b + 16, :] * (1.0 / DEVICES)
        mom = jnp.concatenate([mb[(y - q) % 4, :, cols] for q in range(4)], axis=0)
        base = jnp.concatenate(
            [pick(y, [gb[q, 4 * s : 4 * s + 4, cols] for s in range(4)]) for q in range(4)], axis=0
        )
        new_mom = 0.9 * mom + average
        code[:, cols] = encode(base - 0.7 * (average + 0.9 * new_mom))
        for q in range(4):
            nb[q, :, cols] = new_mom[4 * q : 4 * q + 4, :]
    for d, n in enumerate((n0, n1, n2, n3)):
        n[...] = nb[(y + d) % 4]


def error_kernel(ids, count, g, l, e, out, mask):
    i, j = pl.program_id(0), pl.program_id(1)
    wide = g.shape[1] // BLOCK

    @pl.when((i == 0) & (j == 0))
    def _():
        for n in range(mask.shape[0]):
            mask[n] = jnp.int32(0)
        for k in range(ids.shape[0]):

            @pl.when(k < count[0])
            def _():
                mask[ids[k]] = jnp.int32(1)

    for b in range(wide):
        cols = slice(BLOCK * b, BLOCK * b + BLOCK)
        acc = 0.95 * e[:, cols] + (g[:, cols] - l[:, cols].astype(F32))
        kept = mask[i * 32 + j * wide + b] > 0
        out[:, cols] = acc - jnp.where(kept, acc.astype(BF16).astype(F32), 0.0)


def spread_kernel(pos, g0, g1, g2, g3, s0, s1, s2, s3, n0, n1, n2, n3, out, new_mom, buf, nb, sems):
    y, c, x = pos[0], pos[1], pos[2]
    step = pl.program_id(0)
    core, col = step // 4, step % 4
    copies = [
        [
            pltpu.make_async_copy(src, buf.at[slot, d], sems.at[slot, d])
            for d, src in enumerate(group)
        ]
        for slot, group in ((c, (g0, g1, g2, g3)), (1 - c, (s0, s1, s2, s3)))
    ]

    @pl.when(step == 0)
    def _():
        for group in copies:
            for copy in group:
                copy.start()
        for d, n in enumerate((n0, n1, n2, n3)):
            nb[(y - d) % 4] = n[...]
        for q in range(4):
            new_mom[4 * q : 4 * q + 4, :] = nb[q]

    @pl.when(step % 4 == 0)
    def _():
        for d in range(4):
            pltpu.make_async_copy(g0, buf.at[core, d], sems.at[core, d]).wait()

    dx = (x - col) % 4
    places = []
    for q in range(4):
        dy = (y - q) % 4
        first, second = jnp.where(core == 0, dy, dx), jnp.where(core == 0, dx, dy)
        places.append((first, pl.ds(pl.multiple_of(second * 16, 16), 16)))

    width = 256

    def body(i, _):
        cols = pl.ds(pl.multiple_of(i * width, width), width)
        parts = [decode(buf[core, first, rows, cols]) for first, rows in places]
        for q in range(4):
            out[q, :, cols] = jnp.concatenate([p[4 * q : 4 * q + 4, :] for p in parts], axis=0)
        return 0

    lax.fori_loop(0, out.shape[2] // width, body, 0, unroll=2)


def smem():
    return pl.BlockSpec(memory_space=pltpu.SMEM)


def vmem():
    return pl.BlockSpec(memory_space=pltpu.VMEM)


def hbm():
    return pl.BlockSpec(memory_space=pl.ANY)


def params(mib):
    return pltpu.CompilerParams(vmem_limit_bytes=mib * MIB)


def per_device(global_params, local_params, error_buf, momentum, kept, counts):
    rows, cols = global_params.shape
    local, error = local_params.reshape(rows, cols), error_buf.reshape(rows, cols)
    ids, count = kept.reshape(-1), counts.reshape(-1)
    slots = ids.shape[0]
    y, c, x = place()
    pos = jnp.stack([y, c, x]).astype(jnp.int32)
    sds = jax.ShapeDtypeStruct
    quarter = sds((4, cols), F32)

    pay, m0, m1, m2, m3 = pl.pallas_call(
        pack_kernel,
        out_shape=(sds((DEVICES, 64 + EXTRA, BLOCK), BF16),) + (quarter,) * 4,
        in_specs=[smem(), smem(), smem(), hbm(), hbm(), hbm(), vmem()],
        out_specs=(vmem(),) * 5,
        scratch_shapes=[
            pltpu.VMEM((slots, BLOCK, BLOCK), F32),
            pltpu.VMEM((slots, BLOCK, BLOCK), BF16),
            pltpu.VMEM((slots, BLOCK, BLOCK), F32),
            pltpu.SemaphoreType.DMA((3, slots)),
        ],
        compiler_params=params(16),
        cost_estimate=pl.CostEstimate(flops=2 * MIB, bytes_accessed=4 * MIB, transcendentals=0),
        name="pack",
    )(ids, count, pos, global_params, local, error, momentum)

    m1, m2, m3 = [move(m, lambda y, c, x, d=d: (y + d, c, x)) for d, m in ((1, m1), (2, m2), (3, m3))]
    recv = lax.all_to_all(pay, AXES, 0, 0, tiled=True)

    code, n0, n1, n2, n3 = pl.pallas_call(
        share_kernel,
        out_shape=(sds((16, cols), BF16),) + (quarter,) * 4,
        in_specs=[smem(), vmem(), hbm()] + [vmem()] * 4,
        out_specs=(vmem(),) * 5,
        scratch_shapes=[
            pltpu.VMEM((4, 16, cols), F32),
            pltpu.VMEM((4, 4, cols), F32),
            pltpu.VMEM((4, 4, cols), F32),
            pltpu.SemaphoreType.DMA((4,)),
        ],
        compiler_params=params(16),
        cost_estimate=pl.CostEstimate(flops=256 * MIB, bytes_accessed=4 * MIB, transcendentals=0),
        name="share",
    )(pos, recv, global_params, m0, m1, m2, m3)

    first = [
        move(code, lambda y, c, x, d=d: (y, c, x + d) if c == 0 else (y + d, c, x)) for d in (1, 2, 3)
    ]
    group = jnp.concatenate([code] + first, axis=0)
    own = [group] + [
        move(group, lambda y, c, x, d=d: (y + d, c, x) if c == 0 else (y, c, x + d)) for d in (1, 2, 3)
    ]
    other = [move(g, lambda y, c, x: (y, c + 1, x)) for g in own]
    n1, n2, n3 = [move(n, lambda y, c, x, d=d: (y + d, c, x)) for d, n in ((1, n1), (2, n2), (3, n3))]

    wide = 1024
    spec = pl.BlockSpec((BLOCK, wide), lambda i, j, *_: (i, j))
    new_error = pl.pallas_call(
        error_kernel,
        out_shape=sds((rows, cols), F32),
        grid_spec=pltpu.PrefetchScalarGridSpec(
            num_scalar_prefetch=2,
            grid=(rows // BLOCK, cols // wide),
            in_specs=[spec] * 3,
            out_specs=spec,
            scratch_shapes=[pltpu.SMEM((rows // BLOCK * (cols // BLOCK),), jnp.int32)],
        ),
        compiler_params=params(16),
        cost_estimate=pl.CostEstimate(flops=8 * MIB, bytes_accessed=28 * MIB, transcendentals=0),
        name="error",
    )(ids, count, global_params, local, error)

    new_params, new_momentum = pl.pallas_call(
        spread_kernel,
        out_shape=(sds((4, BLOCK, cols), F32), sds((16, cols), F32)),
        grid=(8,),
        in_specs=[smem()] + [hbm()] * 8 + [vmem()] * 4,
        out_specs=(
            pl.BlockSpec((4, 16, cols), lambda i: (0, i, 0)),
            pl.BlockSpec((16, cols), lambda i: (0, 0)),
        ),
        scratch_shapes=[
            pltpu.VMEM((2, 4, 64, cols), BF16),
            pltpu.VMEM((4, 4, cols), F32),
            pltpu.SemaphoreType.DMA((2, 4)),
        ],
        compiler_params=params(24),
        cost_estimate=pl.CostEstimate(flops=16 * MIB, bytes_accessed=12 * MIB, transcendentals=4 * MIB),
        name="spread",
    )(pos, *own, *other, n0, n1, n2, n3)
    return (
        new_params.reshape(rows, cols),
        new_error.reshape(1, 1, rows, cols),
        new_momentum,
    )


def solution(mesh):
    return jax.shard_map(
        per_device,
        mesh=mesh,
        in_specs=(
            P(None, "tensor"),
            P("region", "island", None, "tensor"),
            P("region", "island", None, "tensor"),
            P(("island", "region"), "tensor"),
            P("region", "island", "tensor", None),
            P("region", "island", "tensor"),
        ),
        out_specs=(
            P(None, "tensor"),
            P("region", "island", None, "tensor"),
            P(("island", "region"), "tensor"),
        ),
        check_vma=False,
    )
```

```python
import functools

import jax
import jax.numpy as jnp
from jax import lax
from jax.experimental import pallas as pl
from jax.experimental.pallas import tpu as pltpu
from jax.sharding import PartitionSpec as P

BLOCK = 128
PARTS = 4
DEVICES = 32
EXTRA = 16
AXES = ("island", "region")
SCALE = 2.0**24
MIB = 2**20
F32 = jnp.float32
BF16 = jnp.bfloat16


def place():
    island = lax.axis_index("island")
    return island // 2, island % 2, lax.axis_index("region")


def move(array, step):
    pairs = []
    for p in range(DEVICES):
        y, c, x = p // 8, p // 4 % 2, p % 4
        y, c, x = step(y, c, x)
        pairs.append((p, 8 * (y % 4) + 4 * (c % 2) + x % 4))
    return lax.ppermute(array, AXES, pairs)


def encode(v):
    v = v * SCALE
    s = v * v
    return jnp.where(v < 0, -(s * s), s * s).astype(BF16)


def decode(code):
    w = code.astype(F32)
    v = lax.rsqrt(lax.rsqrt(jnp.abs(w))) * (1.0 / SCALE)
    return jnp.where(w < 0, -v, v)


def pick(index, choices):
    out = choices[-1]
    for i in range(len(choices) - 2, -1, -1):
        out = jnp.where(index == i, choices[i], out)
    return out


def pack_kernel(ids, count, pos, g, l, e, mom, pay, m0, m1, m2, m3, gb, lb, eb, sems):
    y, x = pos[0], pos[2]
    slots = gb.shape[0]
    copies = []
    for k in range(slots):
        rows = pl.ds(pl.multiple_of(ids[k] // 32 * BLOCK, BLOCK), BLOCK)
        cols = pl.ds(pl.multiple_of(ids[k] % 32 * BLOCK, BLOCK), BLOCK)
        copies.append([
            pltpu.make_async_copy(src.at[rows, cols], dst.at[k], sems.at[i, k])
            for i, (src, dst) in enumerate(((g, gb), (l, lb), (e, eb)))
        ])
        for copy in copies[-1]:
            copy.start()
    for d, out in enumerate((m0, m1, m2, m3)):
        out[...] = pick((y + d) % 4, [mom[4 * q : 4 * q + 4, :] for q in range(4)])
    lane = lax.broadcasted_iota(jnp.int32, (EXTRA, BLOCK), 1)
    vec = jnp.zeros((EXTRA, BLOCK), F32)
    for k in range(slots):
        vec = jnp.where(lane % 64 // 4 == k, ids[k].astype(F32), vec)
    vec = jnp.where(lane // 64 == x % 2, vec, 0.0).astype(BF16)
    for p in range(DEVICES):
        pay[p, 64 : 64 + EXTRA, :] = vec
    for group in range(slots // 4):
        for k in range(4 * group, 4 * group + 4):
            for copy in copies[k]:
                copy.wait()
        for r in range(8):
            rows = slice(16 * r, 16 * r + 16)
            tiles = []
            for k in range(4 * group, 4 * group + 4):
                acc = 0.95 * eb[k, rows, :] + (gb[k, rows, :] - lb[k, rows, :].astype(F32))
                tiles.append(jnp.where(k < count[0], acc, 0.0))
            for q in range(4):
                tile = jnp.concatenate([t[4 * q : 4 * q + 4] for t in tiles], axis=0)
                pay[8 * q + r, 16 * group : 16 * group + 16, :] = tile.astype(BF16)


def share_kernel(pos, recv, g, m0, m1, m2, m3, code, nb, gb, mb, sems):
    y, c, x = pos[0], pos[1], pos[2]
    r = 4 * c + x
    copies = []
    for q in range(4):
        rows = pl.ds(pl.multiple_of(q * BLOCK + 16 * r, 16), 16)
        copies.append(pltpu.make_async_copy(g.at[rows, :], gb.at[q], sems.at[q]))
        copies[-1].start()
    for d, m in enumerate((m0, m1, m2, m3)):
        mb[d] = m[...]
    row = lax.broadcasted_iota(jnp.int32, (512, BLOCK), 0)
    lane = lax.broadcasted_iota(jnp.int32, (512, BLOCK), 1)
    want = (row // 4 % 4 * 32 + row // 16) * 4 + row % 4
    want = (want - lane % 4).astype(F32)
    total = jnp.zeros((512, BLOCK), F32)
    for i in range(0, DEVICES, 4):
        halves = []
        for h in (i, i + 2):
            pair = recv[h, 64 : 64 + EXTRA, :].astype(F32) + recv[h + 1, 64 : 64 + EXTRA, :].astype(F32)
            halves.append((want == 4.0 * pair[0:1, :]).astype(F32).astype(BF16))
        table = jnp.concatenate(halves, axis=1)
        values = jnp.concatenate([recv[i + s, 0:64, :] for s in range(4)], axis=0)
        total = total + jnp.dot(table, values, preferred_element_type=F32)
    for copy in copies:
        copy.wait()
    for b in range(32):
        cols = slice(BLOCK * b, BLOCK * b + BLOCK)
        average = total[16 * b : 16 * b + 16, :] * (1.0 / DEVICES)
        mom = jnp.concatenate([mb[(y - q) % 4, :, cols] for q in range(4)], axis=0)
        base = jnp.concatenate(
            [pick(y, [gb[q, 4 * s : 4 * s + 4, cols] for s in range(4)]) for q in range(4)], axis=0
        )
        new_mom = 0.9 * mom + average
        code[:, cols] = encode(base - 0.7 * (average + 0.9 * new_mom))
        for q in range(4):
            nb[q, :, cols] = new_mom[4 * q : 4 * q + 4, :]


def error_kernel(top, ids, count, g, l, e, *refs):
    out, gb, lb, eb, mask, sems, done = refs[-7:]
    chunks, high, _ = gb.shape
    copies = []
    for i in range(chunks):
        rows = pl.ds(top + i * high, high)
        copies.append([
            pltpu.make_async_copy(src.at[rows, :], dst.at[i], sems.at[n, i])
            for n, (src, dst) in enumerate(((g, gb), (l, lb), (e, eb)))
        ])
        for copy in copies[-1]:
            copy.start()
    for n in range(mask.shape[0]):
        mask[n] = jnp.int32(0)
    for k in range(ids.shape[0]):

        @pl.when(k < count[0])
        def _():
            mask[ids[k]] = jnp.int32(1)

    back = []
    for i in range(chunks):
        for copy in copies[i]:
            copy.wait()
        first = (top + i * high) // BLOCK * 32

        def body(b, _):
            cols = pl.ds(pl.multiple_of(b * BLOCK, BLOCK), BLOCK)
            acc = 0.95 * eb[i, :, cols] + (gb[i, :, cols] - lb[i, :, cols].astype(F32))
            kept = mask[first + b] > 0
            eb[i, :, cols] = acc - jnp.where(kept, acc.astype(BF16).astype(F32), 0.0)
            return 0

        lax.fori_loop(0, 32, body, 0, unroll=4)
        back.append(pltpu.make_async_copy(eb.at[i], out.at[pl.ds(top + i * high, high), :], done.at[i]))
        back[-1].start()
    for copy in back:
        copy.wait()


def spread_kernel(pos, *refs):
    own, other, (out, stage, sems) = refs[:4], refs[4:8], refs[8:]
    y, c, x = pos[0], pos[1], pos[2]
    width = BLOCK

    def unit(slot, tile, parts_of):
        def body(i, _):
            cols = pl.ds(pl.multiple_of(i * width, width), width)
            parts = [decode(part) for part in parts_of(cols)]
            for q in range(4):
                stage[slot, q, :, cols] = jnp.concatenate([p[4 * q : 4 * q + 4, :] for p in parts], axis=0)
            return 0

        lax.fori_loop(0, stage.shape[3] // width, body, 0, unroll=True)
        rows = pl.ds(pl.multiple_of(tile * 16, 16), 16)
        pltpu.make_async_copy(stage.at[slot], out.at[:, rows, :], sems.at[slot]).start()

    def shard(ref, index, cols):
        return ref[pl.ds(pl.multiple_of(index * 16, 16), 16), cols]

    for core in range(2):

        @pl.when(c == core)
        def _():
            groups = own if core == 1 else other
            for d in range(4):
                unit(4 + d, 4 + (x - d) % 4, lambda cols: [shard(groups[d], (y - q) % 4, cols) for q in range(4)])

        groups0 = own if core == 0 else other
        for row in range(4):

            @pl.when((c == core) & (y == row))
            def _():
                def each(d, _):
                    unit(d, (x - d) % 4, lambda cols: [shard(groups0[(row - q) % 4], d, cols) for q in range(4)])
                    return 0

                lax.fori_loop(0, 4, each, 0)

    for slot in range(8):
        pltpu.make_async_copy(stage.at[slot], out.at[:, pl.ds(0, 16), :], sems.at[slot]).wait()


def smem():
    return pl.BlockSpec(memory_space=pltpu.SMEM)


def vmem():
    return pl.BlockSpec(memory_space=pltpu.VMEM)


def hbm():
    return pl.BlockSpec(memory_space=pl.ANY)


def params(mib):
    return pltpu.CompilerParams(vmem_limit_bytes=mib * MIB)


def in_hbm(array):
    return pltpu.with_memory_space_constraint(array, pltpu.HBM)


def error_rows(top, count_rows, high, ids, count, g, l, e, before):
    rows, cols = g.shape
    chunks = count_rows // high
    given = [] if before is None else [before]
    return pl.pallas_call(
        functools.partial(error_kernel, top),
        out_shape=jax.ShapeDtypeStruct((rows, cols), F32),
        in_specs=[smem(), smem()] + [hbm()] * (3 + len(given)),
        out_specs=hbm(),
        input_output_aliases={5: 0} if given else {},
        scratch_shapes=[
            pltpu.VMEM((chunks, high, cols), F32),
            pltpu.VMEM((chunks, high, cols), BF16),
            pltpu.VMEM((chunks, high, cols), F32),
            pltpu.SMEM((rows // BLOCK * (cols // BLOCK),), jnp.int32),
            pltpu.SemaphoreType.DMA((3, chunks)),
            pltpu.SemaphoreType.DMA((chunks,)),
        ],
        compiler_params=params(2 + 10 * count_rows * cols // MIB),
        cost_estimate=pl.CostEstimate(flops=16 * count_rows * cols, bytes_accessed=14 * count_rows * cols, transcendentals=0),
        name=f"error{top}",
    )(ids, count, in_hbm(g), in_hbm(l), in_hbm(e), *given)


def over_y(array):
    return lax.all_to_all(array, "island", 0, 0, axis_index_groups=[[0, 2, 4, 6], [1, 3, 5, 7]], tiled=True)


CUTS = (0, 192, 320, 512)
HIGH = 64


def per_device(global_params, local_params, error_buf, momentum, kept, counts):
    rows, cols = global_params.shape
    local, error = local_params.reshape(rows, cols), error_buf.reshape(rows, cols)
    ids, count = kept.reshape(-1), counts.reshape(-1)
    slots = ids.shape[0]
    y, c, x = place()
    pos = jnp.stack([y, c, x]).astype(jnp.int32)
    sds = jax.ShapeDtypeStruct

    quarter = sds((4, cols), F32)
    pay, m0, m1, m2, m3 = pl.pallas_call(
        pack_kernel,
        out_shape=(sds((DEVICES, 64 + EXTRA, BLOCK), BF16),) + (quarter,) * 4,
        in_specs=[smem(), smem(), smem(), hbm(), hbm(), hbm(), vmem()],
        out_specs=(vmem(),) * 5,
        scratch_shapes=[
            pltpu.VMEM((slots, BLOCK, BLOCK), F32),
            pltpu.VMEM((slots, BLOCK, BLOCK), BF16),
            pltpu.VMEM((slots, BLOCK, BLOCK), F32),
            pltpu.SemaphoreType.DMA((3, slots)),
        ],
        compiler_params=params(16),
        cost_estimate=pl.CostEstimate(flops=2 * MIB, bytes_accessed=4 * MIB, transcendentals=0),
        name="pack",
    )(ids, count, pos, in_hbm(global_params), in_hbm(local), in_hbm(error), momentum)

    m1, m2, m3 = [move(m, lambda y, c, x, d=d: (y + d, c, x)) for d, m in ((1, m1), (2, m2), (3, m3))]
    recv = lax.all_to_all(pay, AXES, 0, 0, tiled=True)
    def part(n, local, before):
        return error_rows(CUTS[n], CUTS[n + 1] - CUTS[n], HIGH, ids, count, global_params, local, error, before)

    pay, local = lax.optimization_barrier((pay, local))
    new_error = part(0, local, None)
    recv, new_error = lax.optimization_barrier((recv, new_error))

    code, new_mom = pl.pallas_call(
        share_kernel,
        out_shape=(sds((16, cols), BF16), sds((4, 4, cols), F32)),
        in_specs=[smem(), vmem(), hbm()] + [vmem()] * 4,
        out_specs=(vmem(),) * 2,
        scratch_shapes=[pltpu.VMEM((4, 16, cols), F32), pltpu.VMEM((4, 4, cols), F32), pltpu.SemaphoreType.DMA((4,))],
        compiler_params=params(16),
        cost_estimate=pl.CostEstimate(flops=256 * MIB, bytes_accessed=4 * MIB, transcendentals=0),
        name="share",
    )(pos, recv, in_hbm(global_params), m0, m1, m2, m3)

    code, local = lax.optimization_barrier((code, local))
    new_error = part(1, local, new_error)
    first = [
        move(code, lambda y, c, x, d=d: (y, c, x + d) if c == 0 else (y + d, c, x)) for d in (1, 2, 3)
    ]
    first, new_error = lax.optimization_barrier((first, new_error))
    group = jnp.concatenate([code] + first, axis=0)
    group, new_mom, local = lax.optimization_barrier((group, new_mom, local))
    own = [
        move(group, lambda y, c, x, d=d: (y + d, c, x) if c == 0 else (y, c, x + d)) for d in (1, 2, 3)
    ]
    new_mom = over_y(new_mom)
    other0 = move(group, lambda y, c, x: (y, c + 1, x))
    new_error = part(2, local, new_error)
    own[0], new_mom, other0, new_error = lax.optimization_barrier((own[0], new_mom, other0, new_error))
    other = [other0] + [move(g, lambda y, c, x: (y, c + 1, x)) for g in own]

    new_params = pl.pallas_call(
        spread_kernel,
        out_shape=sds((4, BLOCK, cols), F32),
        in_specs=[smem()] + [vmem()] * 8,
        out_specs=hbm(),
        scratch_shapes=[pltpu.VMEM((8, 4, 16, cols), F32), pltpu.SemaphoreType.DMA((8,))],
        compiler_params=params(24),
        cost_estimate=pl.CostEstimate(flops=16 * MIB, bytes_accessed=12 * MIB, transcendentals=4 * MIB),
        name="spread",
    )(pos, group, *own, *other)
    return (
        new_params.reshape(rows, cols),
        new_error.reshape(1, 1, rows, cols),
        new_mom.reshape(16, cols),
    )


def solution(mesh):
    return jax.shard_map(
        per_device,
        mesh=mesh,
        in_specs=(
            P(None, "tensor"),
            P("region", "island", None, "tensor"),
            P("region", "island", None, "tensor"),
            P(("island", "region"), "tensor"),
            P("region", "island", "tensor", None),
            P("region", "island", "tensor"),
        ),
        out_specs=(
            P(None, "tensor"),
            P("region", "island", None, "tensor"),
            P(("island", "region"), "tensor"),
        ),
        check_vma=False,
    )
```

```python
import functools

import jax
import jax.numpy as jnp
from jax import lax
from jax.experimental import pallas as pl
from jax.experimental.pallas import tpu as pltpu
from jax.sharding import PartitionSpec as P

BLOCK = 128
PARTS = 4
DEVICES = 32
EXTRA = 8
AXES = ("island", "region")
SCALE = 2.0**24
MIB = 2**20
F32 = jnp.float32
BF16 = jnp.bfloat16


def place():
    island = lax.axis_index("island")
    return island // 2, island % 2, lax.axis_index("region")


def move(array, step):
    pairs = []
    for p in range(DEVICES):
        y, c, x = p // 8, p // 4 % 2, p % 4
        y, c, x = step(y, c, x)
        pairs.append((p, 8 * (y % 4) + 4 * (c % 2) + x % 4))
    return lax.ppermute(array, AXES, pairs)


def encode(v):
    v = v * SCALE
    s = v * v
    return jnp.where(v < 0, -(s * s), s * s).astype(BF16)


def decode(code):
    w = code.astype(F32)
    v = lax.rsqrt(lax.rsqrt(jnp.abs(w))) * (1.0 / SCALE)
    return jnp.where(w < 0, -v, v)


def pick(index, choices):
    out = choices[-1]
    for i in range(len(choices) - 2, -1, -1):
        out = jnp.where(index == i, choices[i], out)
    return out


def pack_kernel(kept, counts, g, l, e, mom, pay, m0, m1, m2, m3, gb, lb, eb, mb, sems, msem):
    y, _, x = place()
    ids = [kept[0, 0, 0, k] for k in range(gb.shape[0])]
    held = pltpu.make_async_copy(mom, mb, msem)
    held.start()
    slots = gb.shape[0]
    copies = []
    for k in range(slots):
        rows = pl.ds(pl.multiple_of(ids[k] // 32 * BLOCK, BLOCK), BLOCK)
        cols = pl.ds(pl.multiple_of(ids[k] % 32 * BLOCK, BLOCK), BLOCK)
        copies.append([
            pltpu.make_async_copy(src.at[rows, cols], dst.at[k], sems.at[i, k])
            for i, (src, dst) in enumerate(((g, gb), (l, lb), (e, eb)))
        ])
        for copy in copies[-1]:
            copy.start()
    lane = lax.broadcasted_iota(jnp.int32, (EXTRA, BLOCK), 1)
    vec = jnp.zeros((EXTRA, BLOCK), F32)
    for k in range(slots):
        vec = jnp.where(lane % 64 // 4 == k, ids[k].astype(F32), vec)
    vec = jnp.where(lane // 64 == x % 2, vec, 0.0).astype(BF16)
    for p in range(DEVICES):
        pay[p, 64 : 64 + EXTRA, :] = vec
    for group in range(slots // 4):
        for k in range(4 * group, 4 * group + 4):
            for copy in copies[k]:
                copy.wait()
        for r in range(8):
            rows = slice(16 * r, 16 * r + 16)
            tiles = []
            for k in range(4 * group, 4 * group + 4):
                acc = 0.95 * eb[k, rows, :] + (gb[k, rows, :] - lb[k, rows, :].astype(F32))
                tiles.append(jnp.where(k < counts[0, 0, 0], acc, 0.0))
            for q in range(4):
                tile = jnp.concatenate([t[4 * q : 4 * q + 4] for t in tiles], axis=0)
                pay[8 * q + r, 16 * group : 16 * group + 16, :] = tile.astype(BF16)
    held.wait()
    for d, out in enumerate((m0, m1, m2, m3)):
        out[...] = pick((y + d) % 4, [mb[4 * q : 4 * q + 4, :] for q in range(4)])


def tiles_of(flat, tall):
    out = []
    if flat is not None:
        cols = flat.shape[1] * 4 // 5
        for t in range(0, cols // 4, BLOCK):
            out.append((None, slice(cols + t, cols + t + BLOCK), [i * cols // 4 + t for i in range(4)]))
    if tall is not None:
        wide = tall.shape[1]
        for k in range(4):
            for t in range(0, wide, BLOCK):
                out.append((slice(16 * k, 16 * k + 16), slice(t, t + BLOCK), [(4 * k + i) * wide + t for i in range(4)]))
    return out


def share_kernel(recv, base, m0, m1, m2, m3, c1, c2, c3, t1, t2, t3, n0, mb, nb):
    y, _, _ = place()
    for d, m in enumerate((m0, m1, m2, m3)):
        mb[d] = m[...]
    row = lax.broadcasted_iota(jnp.int32, (512, BLOCK), 0)
    lane = lax.broadcasted_iota(jnp.int32, (512, BLOCK), 1)
    want = (row // 4 % 4 * 32 + row // 16) * 4 + row % 4
    want = (want - lane % 4).astype(F32)
    total = jnp.zeros((512, BLOCK), F32)
    for i in range(0, DEVICES, 4):
        halves = []
        for h in (i, i + 2):
            pair = recv[h, 64 : 64 + EXTRA, :].astype(F32) + recv[h + 1, 64 : 64 + EXTRA, :].astype(F32)
            halves.append((want == 4.0 * pair[0:1, :]).astype(F32).astype(BF16))
        table = jnp.concatenate(halves, axis=1)
        values = jnp.concatenate([recv[i + s, 0:64, :] for s in range(4)], axis=0)
        total = total + jnp.dot(table, values, preferred_element_type=F32)
    for b in range(32):
        cols = slice(BLOCK * b, BLOCK * b + BLOCK)
        average = total[16 * b : 16 * b + 16, :] * (1.0 / DEVICES)
        mom = jnp.concatenate([mb[(y - q) % 4, :, cols] for q in range(4)], axis=0)
        new_mom = 0.9 * mom + average
        code = encode(base[:, cols] - 0.7 * (average + 0.9 * new_mom))
        for out in (c1, c2, c3):
            out[:, cols] = code
        for q in range(4):
            nb[q, :, cols] = new_mom[4 * q : 4 * q + 4, :]
    n0[...] = nb[y]
    for d, (flat, tall) in enumerate(((c1, t1), (c2, t2), (c3, t3)), 1):
        for rows, cols, places in tiles_of(flat, tall):
            tile = encode(jnp.concatenate([nb[(y + d) % 4, :, p : p + BLOCK] for p in places], axis=0))
            (flat if rows is None else tall)[slice(None) if rows is None else rows, cols] = tile


def group_kernel(c1, r1, r2, r3, t1, t2, t3, g1, g2, g3):
    width = g1.shape[1] - t1.shape[1]
    for n, code in enumerate((c1, r1, r2, r3)):
        part = code[:, :width]
        for out in (g1, g2, g3):
            out[16 * n : 16 * n + 16, :width] = part
    for out, tail in ((g1, t1), (g2, t2), (g3, t3)):
        out[:, width:] = tail[...]


def error_kernel(top, kept, counts, g, l, e, *refs):
    gb, lb, eb, mask, sems, done, rb, rsems = refs[-8:]
    out, base = refs[:2] if top == 0 else (refs[1], None)
    chunks, high, _ = gb.shape
    copies = []
    for i in range(chunks):
        rows = pl.ds(top + i * high, high)
        copies.append([
            pltpu.make_async_copy(src.at[rows, :], dst.at[i], sems.at[n, i])
            for n, (src, dst) in enumerate(((g, gb), (l, lb), (e, eb)))
        ])
        for copy in copies[-1]:
            copy.start()
    if base is not None:
        y, c, x = place()
        reads = []
        for q in range(4):
            rows = pl.ds(pl.multiple_of(q * BLOCK + 16 * (4 * c + x), 16), 16)
            reads.append(pltpu.make_async_copy(g.at[rows, :], rb.at[q], rsems.at[q]))
            reads[-1].start()
    for n in range(mask.shape[0]):
        mask[n] = jnp.int32(0)
    for k in range(kept.shape[-1]):

        @pl.when(k < counts[0, 0, 0])
        def _():
            mask[kept[0, 0, 0, k]] = jnp.int32(1)

    back = []
    for i in range(chunks):
        for copy in copies[i]:
            copy.wait()
        first = (top + i * high) // BLOCK * 32

        def body(b, _):
            cols = pl.ds(pl.multiple_of(b * BLOCK, BLOCK), BLOCK)
            acc = 0.95 * eb[i, :, cols] + (gb[i, :, cols] - lb[i, :, cols].astype(F32))
            kept = mask[first + b] > 0
            eb[i, :, cols] = acc - jnp.where(kept, acc.astype(BF16).astype(F32), 0.0)
            return 0

        lax.fori_loop(0, 32, body, 0, unroll=4)
        back.append(pltpu.make_async_copy(eb.at[i], out.at[pl.ds(top + i * high, high), :], done.at[i]))
        back[-1].start()
    if base is not None:
        for q in range(4):
            reads[q].wait()
            base[4 * q : 4 * q + 4, :] = pick(y, [rb[q, 4 * n : 4 * n + 4, :] for n in range(4)])
    for copy in back:
        copy.wait()


def spread_kernel(early, *refs):
    own, other = refs[:3], refs[3:6]
    wide, half, sems = refs[-3:]
    out = refs[6] if early else refs[11]
    y, c, x = place()
    steps = (0, 1, 3) if early else (1, 2, 3)
    width = BLOCK

    def unit(stage, sem, first, parts_of):
        def body(i, _):
            cols = pl.ds(pl.multiple_of(i * width, width), width)
            parts = [decode(part) for part in parts_of(cols)]
            for q in range(4):
                stage[q, :, cols] = jnp.concatenate([p[4 * q : 4 * q + 4, :] for p in parts], axis=0)
            return 0

        lax.fori_loop(0, stage.shape[2] // width, body, 0, unroll=16)
        rows = pl.ds(pl.multiple_of(first, 8), stage.shape[1])
        pltpu.make_async_copy(stage, out.at[:, rows, :], sem).start()

    def shard(ref, index, cols):
        return ref[pl.ds(pl.multiple_of(index * 16, 16), 16), cols]

    for core in range(2):
        groups = dict(zip(steps, own if core == 1 else other))
        groups0 = dict(zip(steps, own if core == 0 else other))

        @pl.when(c == core)
        def _():
            for n, d in enumerate((0, 1, 3) if early else (2,)):
                first = 16 * (4 + (x - d) % 4)
                unit(wide.at[n], sems.at[n], first, lambda cols: [shard(groups[d], (y - q) % 4, cols) for q in range(4)])

        for row in range(4):
            part = row // 2 if early else 1 - row // 2
            pair = (2 * part, 2 * part + 1)

            @pl.when((c == core) & (y == row))
            def _():
                def each(d, _):
                    first = 16 * ((x - d) % 4) + 8 * part
                    unit(half.at[d], sems.at[3 + d], first, lambda cols: [shard(groups0[(row - q) % 4], d, cols) for q in pair])
                    return 0

                lax.fori_loop(0, 4, each, 0)

    if not early:
        flats, n0, new_mom, nb = refs[7:10], refs[10], refs[12], refs[13]
        nb[y] = n0[...]
        full = nb.shape[2]

        def place_piece(d, ref, first, flat, tall):
            for rows, cols, places in tiles_of(flat, tall):
                cols = slice(cols.start + first, cols.stop + first)
                tile = decode(ref[slice(None) if rows is None else rows, cols])
                for n, p in enumerate(places):
                    nb[(y - d) % 4, :, p : p + BLOCK] = tile[4 * n : 4 * n + 4, :]

        @pl.when(c == 1)
        def _():
            for d, flat in enumerate(flats, 1):
                place_piece(d, flat, 0, flat, None)

        @pl.when(c == 0)
        def _():
            for d, group in enumerate(own, 1):
                place_piece(d, group, full, None, jax.ShapeDtypeStruct((64, full // 16), BF16))

        for q in range(4):
            new_mom[4 * q : 4 * q + 4, :] = nb[q]
    for n in range(wide.shape[0]):
        pltpu.make_async_copy(wide.at[n], out.at[:, pl.ds(0, 16), :], sems.at[n]).wait()
    for d in range(4):
        pltpu.make_async_copy(half.at[d], out.at[:, pl.ds(0, 8), :], sems.at[3 + d]).wait()


def smem():
    return pl.BlockSpec(memory_space=pltpu.SMEM)


def vmem():
    return pl.BlockSpec(memory_space=pltpu.VMEM)


def hbm():
    return pl.BlockSpec(memory_space=pl.ANY)


def params(mib):
    return pltpu.CompilerParams(vmem_limit_bytes=mib * MIB)


def in_hbm(array):
    return pltpu.with_memory_space_constraint(array, pltpu.HBM)


def error_rows(top, count_rows, high, kept, counts, g, l, e, before):
    rows, cols = g.shape
    chunks = count_rows // high
    given = [] if before is None else [before]
    return pl.pallas_call(
        functools.partial(error_kernel, top),
        out_shape=[jax.ShapeDtypeStruct((rows, cols), F32)] + [jax.ShapeDtypeStruct((16, cols), F32)] * (1 - len(given)),
        in_specs=[smem(), smem()] + [hbm()] * (3 + len(given)),
        out_specs=[hbm()] + [vmem()] * (1 - len(given)),
        input_output_aliases={5: 0} if given else {},
        scratch_shapes=[
            pltpu.VMEM((chunks, high, cols), F32),
            pltpu.VMEM((chunks, high, cols), BF16),
            pltpu.VMEM((chunks, high, cols), F32),
            pltpu.SMEM((rows // BLOCK * (cols // BLOCK),), jnp.int32),
            pltpu.SemaphoreType.DMA((3, chunks)),
            pltpu.SemaphoreType.DMA((chunks,)),
            pltpu.VMEM((4, 16, cols), F32),
            pltpu.SemaphoreType.DMA((4,)),
        ],
        compiler_params=params(4 + 10 * count_rows * cols // MIB),
        cost_estimate=pl.CostEstimate(flops=16 * count_rows * cols, bytes_accessed=14 * count_rows * cols, transcendentals=0),
        name=f"error{top}",
    )(kept, counts, in_hbm(g), in_hbm(l), in_hbm(e), *given)


def spread(early, own, other, cols, rest=()):
    sds = jax.ShapeDtypeStruct
    late = not early
    return pl.pallas_call(
        functools.partial(spread_kernel, early),
        out_shape=[sds((4, BLOCK, cols), F32)] + [sds((16, cols), F32)] * late,
        in_specs=[vmem()] * 6 + [hbm()] * late + [vmem()] * (len(rest) - late),
        out_specs=[hbm()] + [vmem()] * late,
        input_output_aliases={6: 0} if late else {},
        scratch_shapes=[pltpu.VMEM((4, 4, cols), F32)] * late
        + [
            pltpu.VMEM((3 if early else 1, 4, 16, cols), F32),
            pltpu.VMEM((4, 4, 8, cols), F32),
            pltpu.SemaphoreType.DMA((7,)),
        ],
        compiler_params=params(24),
        cost_estimate=pl.CostEstimate(
            flops=16 * MIB, bytes_accessed=(8 if early else 5) * MIB, transcendentals=(2 if early else 1) * MIB
        ),
        name="spread_early" if early else "spread_late",
    )(*own, *other, *rest)


CUTS = (0, 192, 320, 384, 512)
HIGH = 64


def per_device(global_params, local_params, error_buf, momentum, kept, counts):
    rows, cols = global_params.shape
    local, error = local_params.reshape(rows, cols), error_buf.reshape(rows, cols)
    slots = kept.shape[-1]
    sds = jax.ShapeDtypeStruct

    quarter = sds((4, cols), F32)
    pay, m0, m1, m2, m3 = pl.pallas_call(
        pack_kernel,
        out_shape=(pltpu.VMEM((DEVICES, 64 + EXTRA, BLOCK), BF16),) + (quarter,) * 4,
        in_specs=[smem(), smem(), hbm(), hbm(), hbm(), hbm()],
        out_specs=(vmem(),) * 5,
        scratch_shapes=[
            pltpu.VMEM((slots, BLOCK, BLOCK), F32),
            pltpu.VMEM((slots, BLOCK, BLOCK), BF16),
            pltpu.VMEM((slots, BLOCK, BLOCK), F32),
            pltpu.VMEM(momentum.shape, F32),
            pltpu.SemaphoreType.DMA((3, slots)),
            pltpu.SemaphoreType.DMA,
        ],
        compiler_params=params(16),
        cost_estimate=pl.CostEstimate(flops=2 * MIB, bytes_accessed=4 * MIB, transcendentals=0),
        name="pack",
    )(kept, counts, in_hbm(global_params), in_hbm(local), in_hbm(error), in_hbm(momentum))

    m1, m2, m3 = [move(m, lambda y, c, x, d=d: (y + d, c, x)) for d, m in ((1, m1), (2, m2), (3, m3))]
    recv = lax.all_to_all(pay, AXES, 0, 0, tiled=True)
    def part(n, local, before):
        return error_rows(CUTS[n], CUTS[n + 1] - CUTS[n], HIGH, kept, counts, global_params, local, error, before)

    pay, local = lax.optimization_barrier((pay, local))
    new_error, base = part(0, local, None)
    recv, new_error, base = lax.optimization_barrier((recv, new_error, base))

    flat, tall = sds((16, cols + cols // 4), BF16), sds((64, cols // 16), BF16)
    *codes, t1, t2, t3, n0 = pl.pallas_call(
        share_kernel,
        out_shape=(flat,) * 3 + (tall,) * 3 + (quarter,),
        in_specs=[vmem()] * 6,
        out_specs=(vmem(),) * 7,
        scratch_shapes=[pltpu.VMEM((4, 4, cols), F32)] * 2,
        compiler_params=params(16),
        cost_estimate=pl.CostEstimate(flops=256 * MIB, bytes_accessed=4 * MIB, transcendentals=0),
        name="share",
    )(recv, base, m0, m1, m2, m3)

    codes[0], local = lax.optimization_barrier((codes[0], local))
    new_error, = part(1, local, new_error)
    first = [
        move(code, lambda y, c, x, d=d: (y, c, x + d) if c == 0 else (y + d, c, x)) for d, code in enumerate(codes, 1)
    ]
    first, new_error = lax.optimization_barrier((first, new_error))
    g1, g2, g3 = pl.pallas_call(
        group_kernel,
        out_shape=(sds((64, cols + cols // 16), BF16),) * 3,
        in_specs=[vmem()] * 7,
        out_specs=(vmem(),) * 3,
        compiler_params=params(16),
        cost_estimate=pl.CostEstimate(flops=0, bytes_accessed=2 * MIB, transcendentals=0),
        name="group",
    )(codes[0], *first, t1, t2, t3)

    def send(group, d):
        return move(group, lambda y, c, x: (y + d, c, x) if c == 0 else (y, c, x + d))

    def swap(group):
        return move(group, lambda y, c, x: (y, c + 1, x))

    g1, local = lax.optimization_barrier((g1, local))
    own1, own3, other0 = send(g1, 1), send(g3, 3), swap(g1)
    new_error, = part(2, local, new_error)
    g2, local, new_error = lax.optimization_barrier((g2, local, new_error))
    own2 = send(g2, 2)
    new_error, = part(3, local, new_error)
    own1, own3, other0, new_error = lax.optimization_barrier((own1, own3, other0, new_error))
    other1, other3 = swap(own1), swap(own3)
    own2, other1, other3 = lax.optimization_barrier((own2, other1, other3))
    other2 = swap(own2)
    new_params, = spread(True, [g1, own1, own3], [other0, other1, other3], cols)
    new_params, new_mom = spread(
        False, [own1, own2, own3], [other1, other2, other3], cols, [new_params, *first, n0]
    )
    return (
        new_params.reshape(rows, cols),
        new_error.reshape(1, 1, rows, cols),
        new_mom,
    )


def solution(mesh):
    return jax.shard_map(
        per_device,
        mesh=mesh,
        in_specs=(
            P(None, "tensor"),
            P("region", "island", None, "tensor"),
            P("region", "island", None, "tensor"),
            P(("island", "region"), "tensor"),
            P("region", "island", "tensor", None),
            P("region", "island", "tensor"),
        ),
        out_specs=(
            P(None, "tensor"),
            P("region", "island", None, "tensor"),
            P(("island", "region"), "tensor"),
        ),
        check_vma=False,
    )
```

```python
import functools

import jax
import jax.numpy as jnp
from jax import lax
from jax.experimental import pallas as pl
from jax.experimental.pallas import tpu as pltpu
from jax.sharding import PartitionSpec as P

BLOCK = 128
PARTS = 4
DEVICES = 32
EXTRA = 8
AXES = ("island", "region")
SCALE = 2.0**24
MIB = 2**20
F32 = jnp.float32
BF16 = jnp.bfloat16


def place():
    island = lax.axis_index("island")
    return island // 2, island % 2, lax.axis_index("region")


def move(array, step):
    pairs = []
    for p in range(DEVICES):
        y, c, x = p // 8, p // 4 % 2, p % 4
        y, c, x = step(y, c, x)
        pairs.append((p, 8 * (y % 4) + 4 * (c % 2) + x % 4))
    return lax.ppermute(array, AXES, pairs)


def encode(v):
    v = v * SCALE
    s = v * v
    return jnp.where(v < 0, -(s * s), s * s).astype(BF16)


def decode(code):
    w = code.astype(F32)
    v = lax.rsqrt(lax.rsqrt(jnp.abs(w))) * (1.0 / SCALE)
    return jnp.where(w < 0, -v, v)


def pick(index, choices):
    out = choices[-1]
    for i in range(len(choices) - 2, -1, -1):
        out = jnp.where(index == i, choices[i], out)
    return out


def pack_kernel(kept, counts, g, l, e, mom, pay, m0, m1, m2, m3, gb, lb, eb, mb, sems, msem):
    y, _, x = place()
    ids = [kept[0, 0, 0, k] for k in range(gb.shape[0])]
    held = pltpu.make_async_copy(mom, mb, msem)
    held.start()
    slots = gb.shape[0]
    copies = []
    for k in range(slots):
        rows = pl.ds(pl.multiple_of(ids[k] // 32 * BLOCK, BLOCK), BLOCK)
        cols = pl.ds(pl.multiple_of(ids[k] % 32 * BLOCK, BLOCK), BLOCK)
        copies.append([
            pltpu.make_async_copy(src.at[rows, cols], dst.at[k], sems.at[i, k])
            for i, (src, dst) in enumerate(((g, gb), (l, lb), (e, eb)))
        ])
        for copy in copies[-1]:
            copy.start()
    lane = lax.broadcasted_iota(jnp.int32, (EXTRA, BLOCK), 1)
    vec = jnp.zeros((EXTRA, BLOCK), F32)
    for k in range(slots):
        vec = jnp.where(lane % 64 // 4 == k, ids[k].astype(F32), vec)
    vec = jnp.where(lane // 64 == x % 2, vec, 0.0).astype(BF16)
    for p in range(DEVICES):
        pay[p, 64 : 64 + EXTRA, :] = vec
    for group in range(slots // 4):
        for k in range(4 * group, 4 * group + 4):
            for copy in copies[k]:
                copy.wait()
        for r in range(8):
            rows = slice(16 * r, 16 * r + 16)
            tiles = []
            for k in range(4 * group, 4 * group + 4):
                acc = 0.95 * eb[k, rows, :] + (gb[k, rows, :] - lb[k, rows, :].astype(F32))
                tiles.append(jnp.where(k < counts[0, 0, 0], acc, 0.0))
            for q in range(4):
                tile = jnp.concatenate([t[4 * q : 4 * q + 4] for t in tiles], axis=0)
                pay[8 * q + r, 16 * group : 16 * group + 16, :] = tile.astype(BF16)
    held.wait()
    for d, out in enumerate((m0, m1, m2, m3)):
        out[...] = pick((y + d) % 4, [mb[4 * q : 4 * q + 4, :] for q in range(4)])


def tiles_of(flat, tall):
    out = []
    if flat is not None:
        cols = flat.shape[1] * 4 // 5
        for t in range(0, cols // 4, BLOCK):
            out.append((None, slice(cols + t, cols + t + BLOCK), [i * cols // 4 + t for i in range(4)]))
    if tall is not None:
        wide = tall.shape[1]
        for k in range(4):
            for t in range(0, wide, BLOCK):
                out.append((slice(16 * k, 16 * k + 16), slice(t, t + BLOCK), [(4 * k + i) * wide + t for i in range(4)]))
    return out


def share_kernel(recv, base, m0, m1, m2, m3, c1, c2, c3, t1, t2, t3, n0, mb, nb):
    y, _, _ = place()
    for d, m in enumerate((m0, m1, m2, m3)):
        mb[d] = m[...]
    row = lax.broadcasted_iota(jnp.int32, (512, BLOCK), 0)
    lane = lax.broadcasted_iota(jnp.int32, (512, BLOCK), 1)
    want = (row // 4 % 4 * 32 + row // 16) * 4 + row % 4
    want = (want - lane % 4).astype(F32)
    total = jnp.zeros((512, BLOCK), F32)
    for i in range(0, DEVICES, 4):
        halves = []
        for h in (i, i + 2):
            pair = recv[h, 64 : 64 + EXTRA, :].astype(F32) + recv[h + 1, 64 : 64 + EXTRA, :].astype(F32)
            halves.append((want == 4.0 * pair[0:1, :]).astype(F32).astype(BF16))
        table = jnp.concatenate(halves, axis=1)
        values = jnp.concatenate([recv[i + s, 0:64, :] for s in range(4)], axis=0)
        total = total + jnp.dot(table, values, preferred_element_type=F32)
    for b in range(32):
        cols = slice(BLOCK * b, BLOCK * b + BLOCK)
        average = total[16 * b : 16 * b + 16, :] * (1.0 / DEVICES)
        mom = jnp.concatenate([mb[(y - q) % 4, :, cols] for q in range(4)], axis=0)
        new_mom = 0.9 * mom + average
        code = encode(base[:, cols] - 0.7 * (average + 0.9 * new_mom))
        for out in (c1, c2, c3):
            out[:, cols] = code
        for q in range(4):
            nb[q, :, cols] = new_mom[4 * q : 4 * q + 4, :]
    n0[...] = nb[y]
    for d, (flat, tall) in enumerate(((c1, t1), (c2, t2), (c3, t3)), 1):
        for rows, cols, places in tiles_of(flat, tall):
            tile = encode(jnp.concatenate([nb[(y + d) % 4, :, p : p + BLOCK] for p in places], axis=0))
            (flat if rows is None else tall)[slice(None) if rows is None else rows, cols] = tile


def group_kernel(c1, r1, r2, r3, t1, t2, t3, g1, g2, g3):
    width = g1.shape[1] - t1.shape[1]
    for n, code in enumerate((c1, r1, r2, r3)):
        part = code[:, :width]
        for out in (g1, g2, g3):
            out[16 * n : 16 * n + 16, :width] = part
    for out, tail in ((g1, t1), (g2, t2), (g3, t3)):
        out[:, width:] = tail[...]


def error_kernel(top, kept, counts, g, l, e, *refs):
    gb, lb, eb, mask, sems, done, rb, rsems = refs[-8:]
    out, base = refs[:2] if top == 0 else (refs[1], None)
    chunks, high, _ = gb.shape
    copies = []
    for i in range(chunks):
        rows = pl.ds(top + i * high, high)
        copies.append([
            pltpu.make_async_copy(src.at[rows, :], dst.at[i], sems.at[n, i])
            for n, (src, dst) in enumerate(((g, gb), (l, lb), (e, eb)))
        ])
        for copy in copies[-1]:
            copy.start()
    if base is not None:
        y, c, x = place()
        reads = []
        for q in range(4):
            rows = pl.ds(pl.multiple_of(q * BLOCK + 16 * (4 * c + x), 16), 16)
            reads.append(pltpu.make_async_copy(g.at[rows, :], rb.at[q], rsems.at[q]))
            reads[-1].start()
    for n in range(mask.shape[0]):
        mask[n] = jnp.int32(0)
    for k in range(kept.shape[-1]):

        @pl.when(k < counts[0, 0, 0])
        def _():
            mask[kept[0, 0, 0, k]] = jnp.int32(1)

    back = []
    for i in range(chunks):
        for copy in copies[i]:
            copy.wait()
        first = (top + i * high) // BLOCK * 32

        def body(b, _):
            cols = pl.ds(pl.multiple_of(b * BLOCK, BLOCK), BLOCK)
            acc = 0.95 * eb[i, :, cols] + (gb[i, :, cols] - lb[i, :, cols].astype(F32))
            kept = mask[first + b] > 0
            eb[i, :, cols] = acc - jnp.where(kept, acc.astype(BF16).astype(F32), 0.0)
            return 0

        lax.fori_loop(0, 32, body, 0, unroll=4)
        back.append(pltpu.make_async_copy(eb.at[i], out.at[pl.ds(top + i * high, high), :], done.at[i]))
        back[-1].start()
    if base is not None:
        for q in range(4):
            reads[q].wait()
            base[4 * q : 4 * q + 4, :] = pick(y, [rb[q, 4 * n : 4 * n + 4, :] for n in range(4)])
    for copy in back:
        copy.wait()


def spread_kernel(mine, *refs):
    groups, (stage, sems) = refs[:4], refs[-2:]
    out = refs[8] if mine else refs[5]
    y, c, x = place()
    half = c if mine else 1 - c
    width = BLOCK

    def unit(slot, tile, parts_of):
        def body(i, _):
            cols = pl.ds(pl.multiple_of(i * width, width), width)
            parts = [decode(part) for part in parts_of(cols)]
            for q in range(4):
                stage[slot, q, :, cols] = jnp.concatenate([p[4 * q : 4 * q + 4, :] for p in parts], axis=0)
            return 0

        lax.fori_loop(0, stage.shape[3] // width, body, 0, unroll=16)
        rows = pl.ds(pl.multiple_of(tile * 16, 16), 16)
        pltpu.make_async_copy(stage.at[slot], out.at[:, rows, :], sems.at[slot]).start()

    def shard(ref, index, cols):
        return ref[pl.ds(pl.multiple_of(index * 16, 16), 16), cols]

    @pl.when(half == 1)
    def _():
        for d in range(4):
            unit(d, 4 + (x - d) % 4, lambda cols: [shard(groups[d], (y - q) % 4, cols) for q in range(4)])

    for row in range(4):

        @pl.when((half == 0) & (y == row))
        def _():
            def each(d, _):
                unit(d, (x - d) % 4, lambda cols: [shard(groups[(row - q) % 4], d, cols) for q in range(4)])
                return 0

            lax.fori_loop(0, 4, each, 0)

    if mine:
        flats, n0, new_mom, nb = refs[4:7], refs[7], refs[9], refs[10]
        nb[y] = n0[...]
        full = nb.shape[2]

        def place_piece(d, ref, first, flat, tall):
            for rows, cols, places in tiles_of(flat, tall):
                cols = slice(cols.start + first, cols.stop + first)
                tile = decode(ref[slice(None) if rows is None else rows, cols])
                for n, p in enumerate(places):
                    nb[(y - d) % 4, :, p : p + BLOCK] = tile[4 * n : 4 * n + 4, :]

        @pl.when(c == 1)
        def _():
            for d, flat in enumerate(flats, 1):
                place_piece(d, flat, 0, flat, None)

        @pl.when(c == 0)
        def _():
            for d, group in enumerate(groups[1:], 1):
                place_piece(d, group, full, None, jax.ShapeDtypeStruct((64, full // 16), BF16))

        for q in range(4):
            new_mom[4 * q : 4 * q + 4, :] = nb[q]
    for slot in range(4):
        pltpu.make_async_copy(stage.at[slot], out.at[:, pl.ds(0, 16), :], sems.at[slot]).wait()


def smem():
    return pl.BlockSpec(memory_space=pltpu.SMEM)


def vmem():
    return pl.BlockSpec(memory_space=pltpu.VMEM)


def hbm():
    return pl.BlockSpec(memory_space=pl.ANY)


def params(mib):
    return pltpu.CompilerParams(vmem_limit_bytes=mib * MIB)


def in_hbm(array):
    return pltpu.with_memory_space_constraint(array, pltpu.HBM)


def error_rows(top, count_rows, high, kept, counts, g, l, e, before):
    rows, cols = g.shape
    chunks = count_rows // high
    given = [] if before is None else [before]
    return pl.pallas_call(
        functools.partial(error_kernel, top),
        out_shape=[jax.ShapeDtypeStruct((rows, cols), F32)] + [jax.ShapeDtypeStruct((16, cols), F32)] * (1 - len(given)),
        in_specs=[smem(), smem()] + [hbm()] * (3 + len(given)),
        out_specs=[hbm()] + [vmem()] * (1 - len(given)),
        input_output_aliases={5: 0} if given else {},
        scratch_shapes=[
            pltpu.VMEM((chunks, high, cols), F32),
            pltpu.VMEM((chunks, high, cols), BF16),
            pltpu.VMEM((chunks, high, cols), F32),
            pltpu.SMEM((rows // BLOCK * (cols // BLOCK),), jnp.int32),
            pltpu.SemaphoreType.DMA((3, chunks)),
            pltpu.SemaphoreType.DMA((chunks,)),
            pltpu.VMEM((4, 16, cols), F32),
            pltpu.SemaphoreType.DMA((4,)),
        ],
        compiler_params=params(4 + 10 * count_rows * cols // MIB),
        cost_estimate=pl.CostEstimate(flops=16 * count_rows * cols, bytes_accessed=14 * count_rows * cols, transcendentals=0),
        name=f"error{top}",
    )(kept, counts, in_hbm(g), in_hbm(l), in_hbm(e), *given)


def spread(groups, cols, before=None, rest=()):
    sds = jax.ShapeDtypeStruct
    mine = before is None
    return pl.pallas_call(
        functools.partial(spread_kernel, mine),
        out_shape=[sds((4, BLOCK, cols), F32)] + [sds((16, cols), F32)] * mine,
        in_specs=[vmem()] * (4 + len(rest)) + [hbm()] * (1 - mine),
        out_specs=[hbm()] + [vmem()] * mine,
        input_output_aliases={} if mine else {4: 0},
        scratch_shapes=[pltpu.VMEM((4, 4, cols), F32)] * mine
        + [pltpu.VMEM((4, 4, 16, cols), F32), pltpu.SemaphoreType.DMA((4,))],
        compiler_params=params(16),
        cost_estimate=pl.CostEstimate(flops=8 * MIB, bytes_accessed=6 * MIB, transcendentals=2 * MIB),
        name="spread_mine" if mine else "spread_other",
    )(*groups, *rest, *([] if mine else [before]))


CUTS = (0, 256, 320, 512)
HIGH = 64


def per_device(global_params, local_params, error_buf, momentum, kept, counts):
    rows, cols = global_params.shape
    local, error = local_params.reshape(rows, cols), error_buf.reshape(rows, cols)
    slots = kept.shape[-1]
    sds = jax.ShapeDtypeStruct

    quarter = sds((4, cols), F32)
    pay, m0, m1, m2, m3 = pl.pallas_call(
        pack_kernel,
        out_shape=(pltpu.VMEM((DEVICES, 64 + EXTRA, BLOCK), BF16),) + (quarter,) * 4,
        in_specs=[smem(), smem(), hbm(), hbm(), hbm(), hbm()],
        out_specs=(vmem(),) * 5,
        scratch_shapes=[
            pltpu.VMEM((slots, BLOCK, BLOCK), F32),
            pltpu.VMEM((slots, BLOCK, BLOCK), BF16),
            pltpu.VMEM((slots, BLOCK, BLOCK), F32),
            pltpu.VMEM(momentum.shape, F32),
            pltpu.SemaphoreType.DMA((3, slots)),
            pltpu.SemaphoreType.DMA,
        ],
        compiler_params=params(16),
        cost_estimate=pl.CostEstimate(flops=2 * MIB, bytes_accessed=4 * MIB, transcendentals=0),
        name="pack",
    )(kept, counts, in_hbm(global_params), in_hbm(local), in_hbm(error), in_hbm(momentum))

    m1, m2, m3 = [move(m, lambda y, c, x, d=d: (y + d, c, x)) for d, m in ((1, m1), (2, m2), (3, m3))]
    recv = lax.all_to_all(pay, AXES, 0, 0, tiled=True)
    def part(n, local, before):
        return error_rows(CUTS[n], CUTS[n + 1] - CUTS[n], HIGH, kept, counts, global_params, local, error, before)

    pay, local = lax.optimization_barrier((pay, local))
    new_error, base = part(0, local, None)
    recv, new_error, base = lax.optimization_barrier((recv, new_error, base))

    flat, tall = sds((16, cols + cols // 4), BF16), sds((64, cols // 16), BF16)
    *codes, t1, t2, t3, n0 = pl.pallas_call(
        share_kernel,
        out_shape=(flat,) * 3 + (tall,) * 3 + (quarter,),
        in_specs=[vmem()] * 6,
        out_specs=(vmem(),) * 7,
        scratch_shapes=[pltpu.VMEM((4, 4, cols), F32)] * 2,
        compiler_params=params(16),
        cost_estimate=pl.CostEstimate(flops=256 * MIB, bytes_accessed=4 * MIB, transcendentals=0),
        name="share",
    )(recv, base, m0, m1, m2, m3)

    codes[0], local = lax.optimization_barrier((codes[0], local))
    new_error, = part(1, local, new_error)
    first = [
        move(code, lambda y, c, x, d=d: (y, c, x + d) if c == 0 else (y + d, c, x)) for d, code in enumerate(codes, 1)
    ]
    first, new_error = lax.optimization_barrier((first, new_error))
    g1, g2, g3 = pl.pallas_call(
        group_kernel,
        out_shape=(sds((64, cols + cols // 16), BF16),) * 3,
        in_specs=[vmem()] * 7,
        out_specs=(vmem(),) * 3,
        compiler_params=params(16),
        cost_estimate=pl.CostEstimate(flops=0, bytes_accessed=2 * MIB, transcendentals=0),
        name="group",
    )(codes[0], *first, t1, t2, t3)

    def send(group, d):
        return move(group, lambda y, c, x: (y + d, c, x) if c == 0 else (y, c, x + d))

    def swap(group):
        return move(group, lambda y, c, x: (y, c + 1, x))

    g1, g2, g3, local = lax.optimization_barrier((g1, g2, g3, local))
    own = [g1] + [send(g, d) for d, g in enumerate((g1, g2, g3), 1)]
    new_error, = part(2, local, new_error)
    own, new_error = lax.optimization_barrier((own, new_error))
    other = [swap(g) for g in own]
    new_params, new_mom = spread(own, cols, None, [*first, n0])
    new_params, = spread(other, cols, new_params)
    return (
        new_params.reshape(rows, cols),
        new_error.reshape(1, 1, rows, cols),
        new_mom,
    )


def solution(mesh):
    return jax.shard_map(
        per_device,
        mesh=mesh,
        in_specs=(
            P(None, "tensor"),
            P("region", "island", None, "tensor"),
            P("region", "island", None, "tensor"),
            P(("island", "region"), "tensor"),
            P("region", "island", "tensor", None),
            P("region", "island", "tensor"),
        ),
        out_specs=(
            P(None, "tensor"),
            P("region", "island", None, "tensor"),
            P(("island", "region"), "tensor"),
        ),
        check_vma=False,
    )
```

```python
import functools

import jax
import jax.numpy as jnp
from jax import lax
from jax.experimental import pallas as pl
from jax.experimental.pallas import tpu as pltpu
from jax.sharding import PartitionSpec as P

BLOCK = 128
PARTS = 4
DEVICES = 32
EXTRA = 8
AXES = ("island", "region")
SCALE = 2.0**24
MIB = 2**20
F32 = jnp.float32
BF16 = jnp.bfloat16


def place():
    island = lax.axis_index("island")
    return island // 2, island % 2, lax.axis_index("region")


def move(array, step):
    pairs = []
    for p in range(DEVICES):
        y, c, x = p // 8, p // 4 % 2, p % 4
        y, c, x = step(y, c, x)
        pairs.append((p, 8 * (y % 4) + 4 * (c % 2) + x % 4))
    return lax.ppermute(array, AXES, pairs)


def encode(v):
    v = v * SCALE
    s = v * v
    return jnp.where(v < 0, -(s * s), s * s).astype(BF16)


def decode(code):
    w = code.astype(F32)
    return lax.rsqrt(lax.rsqrt(jnp.abs(w))) * jnp.where(w < 0, -1.0 / SCALE, 1.0 / SCALE)


def pick(index, choices):
    out = choices[-1]
    for i in range(len(choices) - 2, -1, -1):
        out = jnp.where(index == i, choices[i], out)
    return out


def pack_kernel(kept, counts, g, l, e, mom, pay, m0, m1, m2, m3, gb, lb, eb, mb, sems, msem):
    y, _, x = place()
    ids = [kept[0, 0, 0, k] for k in range(gb.shape[0])]
    held = pltpu.make_async_copy(mom, mb, msem)
    held.start()
    slots = gb.shape[0]
    copies = []
    for k in range(slots):
        rows = pl.ds(pl.multiple_of(ids[k] // 32 * BLOCK, BLOCK), BLOCK)
        cols = pl.ds(pl.multiple_of(ids[k] % 32 * BLOCK, BLOCK), BLOCK)
        copies.append([
            pltpu.make_async_copy(src.at[rows, cols], dst.at[k], sems.at[i, k])
            for i, (src, dst) in enumerate(((g, gb), (l, lb), (e, eb)))
        ])
        for copy in copies[-1]:
            copy.start()
    lane = lax.broadcasted_iota(jnp.int32, (EXTRA, BLOCK), 1)
    vec = jnp.zeros((EXTRA, BLOCK), F32)
    for k in range(slots):
        vec = jnp.where(lane % 64 // 4 == k, ids[k].astype(F32), vec)
    vec = jnp.where(lane // 64 == x % 2, vec, 0.0).astype(BF16)
    for p in range(DEVICES):
        pay[p, 64 : 64 + EXTRA, :] = vec
    for group in range(slots // 4):
        for k in range(4 * group, 4 * group + 4):
            for copy in copies[k]:
                copy.wait()
        for r in range(8):
            rows = slice(16 * r, 16 * r + 16)
            tiles = []
            for k in range(4 * group, 4 * group + 4):
                acc = 0.95 * eb[k, rows, :] + (gb[k, rows, :] - lb[k, rows, :].astype(F32))
                tiles.append(jnp.where(k < counts[0, 0, 0], acc, 0.0))
            for q in range(4):
                tile = jnp.concatenate([t[4 * q : 4 * q + 4] for t in tiles], axis=0)
                pay[8 * q + r, 16 * group : 16 * group + 16, :] = tile.astype(BF16)
    held.wait()
    for d, out in enumerate((m0, m1, m2, m3)):
        out[...] = pick((y + d) % 4, [mb[4 * q : 4 * q + 4, :] for q in range(4)])


def tiles_of(flat, tall):
    out = []
    if flat is not None:
        cols = flat.shape[1] * 4 // 5
        for t in range(0, cols // 4, BLOCK):
            out.append((None, slice(cols + t, cols + t + BLOCK), [i * cols // 4 + t for i in range(4)]))
    if tall is not None:
        wide = tall.shape[1]
        for k in range(4):
            for t in range(0, wide, BLOCK):
                out.append((slice(16 * k, 16 * k + 16), slice(t, t + BLOCK), [(4 * k + i) * wide + t for i in range(4)]))
    return out


def share_kernel(recv, base, m0, m1, m2, m3, c1, c2, c3, t1, t2, t3, n0, mb, nb):
    y, _, _ = place()
    for d, m in enumerate((m0, m1, m2, m3)):
        mb[d] = m[...]
    row = lax.broadcasted_iota(jnp.int32, (512, BLOCK), 0)
    lane = lax.broadcasted_iota(jnp.int32, (512, BLOCK), 1)
    want = (row // 4 % 4 * 32 + row // 16) * 4 + row % 4
    want = (want - lane % 4).astype(F32)
    total = jnp.zeros((512, BLOCK), F32)
    for i in range(0, DEVICES, 4):
        halves = []
        for h in (i, i + 2):
            pair = recv[h, 64 : 64 + EXTRA, :].astype(F32) + recv[h + 1, 64 : 64 + EXTRA, :].astype(F32)
            halves.append((want == 4.0 * pair[0:1, :]).astype(F32).astype(BF16))
        table = jnp.concatenate(halves, axis=1)
        values = jnp.concatenate([recv[i + s, 0:64, :] for s in range(4)], axis=0)
        total = total + jnp.dot(table, values, preferred_element_type=F32)
    for b in range(32):
        cols = slice(BLOCK * b, BLOCK * b + BLOCK)
        average = total[16 * b : 16 * b + 16, :] * (1.0 / DEVICES)
        mom = jnp.concatenate([mb[(y - q) % 4, :, cols] for q in range(4)], axis=0)
        new_mom = 0.9 * mom + average
        code = encode(base[:, cols] - 0.7 * (average + 0.9 * new_mom))
        for out in (c1, c2, c3):
            out[:, cols] = code
        for q in range(4):
            nb[q, :, cols] = new_mom[4 * q : 4 * q + 4, :]
    n0[...] = nb[y]
    for d, (flat, tall) in enumerate(((c1, t1), (c2, t2), (c3, t3)), 1):
        for rows, cols, places in tiles_of(flat, tall):
            tile = encode(jnp.concatenate([nb[(y + d) % 4, :, p : p + BLOCK] for p in places], axis=0))
            (flat if rows is None else tall)[slice(None) if rows is None else rows, cols] = tile


def group_kernel(c1, r1, r2, r3, t1, t2, t3, g1, g2, g3):
    width = g1.shape[1] - t1.shape[1]
    for n, code in enumerate((c1, r1, r2, r3)):
        part = code[:, :width]
        for out in (g1, g2, g3):
            out[16 * n : 16 * n + 16, :width] = part
    for out, tail in ((g1, t1), (g2, t2), (g3, t3)):
        out[:, width:] = tail[...]


def error_kernel(top, kept, counts, g, l, e, *refs):
    gb, lb, eb, mask, sems, done, rb, rsems = refs[-8:]
    out, base = refs[:2] if top == 0 else (refs[1], None)
    chunks, high, _ = gb.shape
    copies = []
    for i in range(chunks):
        rows = pl.ds(top + i * high, high)
        copies.append([
            pltpu.make_async_copy(src.at[rows, :], dst.at[i], sems.at[n, i])
            for n, (src, dst) in enumerate(((g, gb), (l, lb), (e, eb)))
        ])
        for copy in copies[-1]:
            copy.start()
    if base is not None:
        y, c, x = place()
        reads = []
        for q in range(4):
            rows = pl.ds(pl.multiple_of(q * BLOCK + 16 * (4 * c + x), 16), 16)
            reads.append(pltpu.make_async_copy(g.at[rows, :], rb.at[q], rsems.at[q]))
            reads[-1].start()
    for n in range(mask.shape[0]):
        mask[n] = jnp.int32(0)
    for k in range(kept.shape[-1]):

        @pl.when(k < counts[0, 0, 0])
        def _():
            mask[kept[0, 0, 0, k]] = jnp.int32(1)

    back = []
    for i in range(chunks):
        for copy in copies[i]:
            copy.wait()
        first = (top + i * high) // BLOCK * 32

        def body(b, _):
            cols = pl.ds(pl.multiple_of(b * BLOCK, BLOCK), BLOCK)
            acc = 0.95 * eb[i, :, cols] + (gb[i, :, cols] - lb[i, :, cols].astype(F32))
            kept = mask[first + b] > 0
            eb[i, :, cols] = acc - jnp.where(kept, acc.astype(BF16).astype(F32), 0.0)
            return 0

        lax.fori_loop(0, 32, body, 0, unroll=4)
        back.append(pltpu.make_async_copy(eb.at[i], out.at[pl.ds(top + i * high, high), :], done.at[i]))
        back[-1].start()
    if base is not None:
        for q in range(4):
            reads[q].wait()
            base[4 * q : 4 * q + 4, :] = pick(y, [rb[q, 4 * n : 4 * n + 4, :] for n in range(4)])
    for copy in back:
        copy.wait()


def spread_kernel(mine, *refs):
    groups, (stage, sems) = refs[:4], refs[-2:]
    out = refs[8] if mine else refs[5]
    y, c, x = place()
    half = c if mine else 1 - c
    width = BLOCK

    def unit(slot, tile, parts_of):
        def body(i, _):
            cols = pl.ds(pl.multiple_of(i * width, width), width)
            parts = [decode(part) for part in parts_of(cols)]
            for q in range(4):
                stage[slot, q, :, cols] = jnp.concatenate([p[4 * q : 4 * q + 4, :] for p in parts], axis=0)
            return 0

        rows = pl.ds(pl.multiple_of(tile * 16, 16), 16)
        part = stage.shape[3] // PIECES
        for n in range(PIECES):
            lax.fori_loop(n * part // width, (n + 1) * part // width, body, 0, unroll=True)
            cols = pl.ds(n * part, part)
            pltpu.make_async_copy(stage.at[slot, :, :, cols], out.at[:, rows, cols], sems.at[slot]).start()

    def shard(ref, index, cols):
        return ref[pl.ds(pl.multiple_of(index * 16, 16), 16), cols]

    @pl.when(half == 1)
    def _():
        for d in range(4):
            unit(d, 4 + (x - d) % 4, lambda cols: [shard(groups[d], (y - q) % 4, cols) for q in range(4)])

    for row in range(4):

        @pl.when((half == 0) & (y == row))
        def _():
            def each(d, _):
                unit(d, (x - d) % 4, lambda cols: [shard(groups[(row - q) % 4], d, cols) for q in range(4)])
                return 0

            lax.fori_loop(0, 4, each, 0)

    if mine:
        flats, n0, new_mom, nb = refs[4:7], refs[7], refs[9], refs[10]
        nb[y] = n0[...]
        full = nb.shape[2]

        def place_piece(d, ref, first, flat, tall):
            for rows, cols, places in tiles_of(flat, tall):
                cols = slice(cols.start + first, cols.stop + first)
                tile = decode(ref[slice(None) if rows is None else rows, cols])
                for n, p in enumerate(places):
                    nb[(y - d) % 4, :, p : p + BLOCK] = tile[4 * n : 4 * n + 4, :]

        @pl.when(c == 1)
        def _():
            for d, flat in enumerate(flats, 1):
                place_piece(d, flat, 0, flat, None)

        @pl.when(c == 0)
        def _():
            for d, group in enumerate(groups[1:], 1):
                place_piece(d, group, full, None, jax.ShapeDtypeStruct((64, full // 16), BF16))

        for q in range(4):
            new_mom[4 * q : 4 * q + 4, :] = nb[q]
    for slot in range(4):
        pltpu.make_async_copy(stage.at[slot], out.at[:, pl.ds(0, 16), :], sems.at[slot]).wait()


def smem():
    return pl.BlockSpec(memory_space=pltpu.SMEM)


def vmem():
    return pl.BlockSpec(memory_space=pltpu.VMEM)


def hbm():
    return pl.BlockSpec(memory_space=pl.ANY)


def params(mib):
    return pltpu.CompilerParams(vmem_limit_bytes=mib * MIB)


def in_hbm(array):
    return pltpu.with_memory_space_constraint(array, pltpu.HBM)


def error_rows(top, count_rows, high, kept, counts, g, l, e, before):
    rows, cols = g.shape
    chunks = count_rows // high
    given = [] if before is None else [before]
    return pl.pallas_call(
        functools.partial(error_kernel, top),
        out_shape=[jax.ShapeDtypeStruct((rows, cols), F32)] + [jax.ShapeDtypeStruct((16, cols), F32)] * (1 - len(given)),
        in_specs=[smem(), smem()] + [hbm()] * (3 + len(given)),
        out_specs=[hbm()] + [vmem()] * (1 - len(given)),
        input_output_aliases={5: 0} if given else {},
        scratch_shapes=[
            pltpu.VMEM((chunks, high, cols), F32),
            pltpu.VMEM((chunks, high, cols), BF16),
            pltpu.VMEM((chunks, high, cols), F32),
            pltpu.SMEM((rows // BLOCK * (cols // BLOCK),), jnp.int32),
            pltpu.SemaphoreType.DMA((3, chunks)),
            pltpu.SemaphoreType.DMA((chunks,)),
            pltpu.VMEM((4, 16, cols), F32),
            pltpu.SemaphoreType.DMA((4,)),
        ],
        compiler_params=params(4 + 10 * count_rows * cols // MIB),
        cost_estimate=pl.CostEstimate(flops=16 * count_rows * cols, bytes_accessed=14 * count_rows * cols, transcendentals=0),
        name=f"error{top}",
    )(kept, counts, in_hbm(g), in_hbm(l), in_hbm(e), *given)


def spread(groups, cols, before=None, rest=()):
    sds = jax.ShapeDtypeStruct
    mine = before is None
    return pl.pallas_call(
        functools.partial(spread_kernel, mine),
        out_shape=[sds((4, BLOCK, cols), F32)] + [sds((16, cols), F32)] * mine,
        in_specs=[vmem()] * (4 + len(rest)) + [hbm()] * (1 - mine),
        out_specs=[hbm()] + [vmem()] * mine,
        input_output_aliases={} if mine else {4: 0},
        scratch_shapes=[pltpu.VMEM((4, 4, cols), F32)] * mine
        + [pltpu.VMEM((4, 4, 16, cols), F32), pltpu.SemaphoreType.DMA((4,))],
        compiler_params=params(16),
        cost_estimate=pl.CostEstimate(flops=8 * MIB, bytes_accessed=6 * MIB, transcendentals=2 * MIB),
        name="spread_mine" if mine else "spread_other",
    )(*groups, *rest, *([] if mine else [before]))


CUTS = (0, 256, 320, 512)
HIGH = 64
PIECES = 4


def per_device(global_params, local_params, error_buf, momentum, kept, counts):
    rows, cols = global_params.shape
    local, error = local_params.reshape(rows, cols), error_buf.reshape(rows, cols)
    slots = kept.shape[-1]
    sds = jax.ShapeDtypeStruct

    quarter = sds((4, cols), F32)
    pay, m0, m1, m2, m3 = pl.pallas_call(
        pack_kernel,
        out_shape=(pltpu.VMEM((DEVICES, 64 + EXTRA, BLOCK), BF16),) + (quarter,) * 4,
        in_specs=[smem(), smem(), hbm(), hbm(), hbm(), hbm()],
        out_specs=(vmem(),) * 5,
        scratch_shapes=[
            pltpu.VMEM((slots, BLOCK, BLOCK), F32),
            pltpu.VMEM((slots, BLOCK, BLOCK), BF16),
            pltpu.VMEM((slots, BLOCK, BLOCK), F32),
            pltpu.VMEM(momentum.shape, F32),
            pltpu.SemaphoreType.DMA((3, slots)),
            pltpu.SemaphoreType.DMA,
        ],
        compiler_params=params(16),
        cost_estimate=pl.CostEstimate(flops=2 * MIB, bytes_accessed=4 * MIB, transcendentals=0),
        name="pack",
    )(kept, counts, in_hbm(global_params), in_hbm(local), in_hbm(error), in_hbm(momentum))

    m1, m2, m3 = [move(m, lambda y, c, x, d=d: (y + d, c, x)) for d, m in ((1, m1), (2, m2), (3, m3))]
    recv = lax.all_to_all(pay, AXES, 0, 0, tiled=True)
    def part(n, local, before):
        return error_rows(CUTS[n], CUTS[n + 1] - CUTS[n], HIGH, kept, counts, global_params, local, error, before)

    pay, local = lax.optimization_barrier((pay, local))
    new_error, base = part(0, local, None)
    recv, new_error, base = lax.optimization_barrier((recv, new_error, base))

    flat, tall = sds((16, cols + cols // 4), BF16), sds((64, cols // 16), BF16)
    *codes, t1, t2, t3, n0 = pl.pallas_call(
        share_kernel,
        out_shape=(flat,) * 3 + (tall,) * 3 + (quarter,),
        in_specs=[vmem()] * 6,
        out_specs=(vmem(),) * 7,
        scratch_shapes=[pltpu.VMEM((4, 4, cols), F32)] * 2,
        compiler_params=params(16),
        cost_estimate=pl.CostEstimate(flops=256 * MIB, bytes_accessed=4 * MIB, transcendentals=0),
        name="share",
    )(recv, base, m0, m1, m2, m3)

    codes[0], local = lax.optimization_barrier((codes[0], local))
    new_error, = part(1, local, new_error)
    first = [
        move(code, lambda y, c, x, d=d: (y, c, x + d) if c == 0 else (y + d, c, x)) for d, code in enumerate(codes, 1)
    ]
    first, new_error = lax.optimization_barrier((first, new_error))
    g1, g2, g3 = pl.pallas_call(
        group_kernel,
        out_shape=(sds((64, cols + cols // 16), BF16),) * 3,
        in_specs=[vmem()] * 7,
        out_specs=(vmem(),) * 3,
        compiler_params=params(16),
        cost_estimate=pl.CostEstimate(flops=0, bytes_accessed=2 * MIB, transcendentals=0),
        name="group",
    )(codes[0], *first, t1, t2, t3)

    def send(group, d):
        return move(group, lambda y, c, x: (y + d, c, x) if c == 0 else (y, c, x + d))

    def swap(group):
        return move(group, lambda y, c, x: (y, c + 1, x))

    g1, g2, g3, local = lax.optimization_barrier((g1, g2, g3, local))
    own = [g1] + [send(g, d) for d, g in enumerate((g1, g2, g3), 1)]
    new_error, = part(2, local, new_error)
    own, new_error = lax.optimization_barrier((own, new_error))
    other = [swap(g) for g in own]
    new_params, new_mom = spread(own, cols, None, [*first, n0])
    new_params, = spread(other, cols, new_params)
    return (
        new_params.reshape(rows, cols),
        new_error.reshape(1, 1, rows, cols),
        new_mom,
    )


def solution(mesh):
    return jax.shard_map(
        per_device,
        mesh=mesh,
        in_specs=(
            P(None, "tensor"),
            P("region", "island", None, "tensor"),
            P("region", "island", None, "tensor"),
            P(("island", "region"), "tensor"),
            P("region", "island", "tensor", None),
            P("region", "island", "tensor"),
        ),
        out_specs=(
            P(None, "tensor"),
            P("region", "island", None, "tensor"),
            P(("island", "region"), "tensor"),
        ),
        check_vma=False,
    )
```

```python
import functools

import jax
import jax.numpy as jnp
from jax import lax
from jax.experimental import pallas as pl
from jax.experimental.pallas import tpu as pltpu
from jax.sharding import PartitionSpec as P

BLOCK = 128
PARTS = 4
DEVICES = 32
EXTRA = 8
AXES = ("island", "region")
SCALE = 2.0**24
MIB = 2**20
F32 = jnp.float32
BF16 = jnp.bfloat16


def place():
    island = lax.axis_index("island")
    return island // 2, island % 2, lax.axis_index("region")


def move(array, step):
    pairs = []
    for p in range(DEVICES):
        y, c, x = p // 8, p // 4 % 2, p % 4
        y, c, x = step(y, c, x)
        pairs.append((p, 8 * (y % 4) + 4 * (c % 2) + x % 4))
    return lax.ppermute(array, AXES, pairs)


def encode(v):
    v = v * SCALE
    s = v * v
    return jnp.where(v < 0, -(s * s), s * s).astype(BF16)


def decode(code):
    w = code.astype(F32)
    return lax.rsqrt(lax.rsqrt(jnp.abs(w))) * jnp.where(w < 0, -1.0 / SCALE, 1.0 / SCALE)


def pick(index, choices):
    out = choices[-1]
    for i in range(len(choices) - 2, -1, -1):
        out = jnp.where(index == i, choices[i], out)
    return out


def pack_kernel(kept, counts, g, l, e, mom, pay, m0, m1, m2, m3, gb, lb, eb, mb, sems, msem):
    y, _, x = place()
    ids = [kept[0, 0, 0, k] for k in range(gb.shape[0])]
    held = pltpu.make_async_copy(mom, mb, msem)
    held.start()
    slots = gb.shape[0]
    copies = []
    for k in range(slots):
        rows = pl.ds(pl.multiple_of(ids[k] // 32 * BLOCK, BLOCK), BLOCK)
        cols = pl.ds(pl.multiple_of(ids[k] % 32 * BLOCK, BLOCK), BLOCK)
        copies.append([
            pltpu.make_async_copy(src.at[rows, cols], dst.at[k], sems.at[i, k])
            for i, (src, dst) in enumerate(((g, gb), (l, lb), (e, eb)))
        ])
        for copy in copies[-1]:
            copy.start()
    lane = lax.broadcasted_iota(jnp.int32, (EXTRA, BLOCK), 1)
    vec = jnp.zeros((EXTRA, BLOCK), F32)
    for k in range(slots):
        vec = jnp.where(lane % 64 // 4 == k, ids[k].astype(F32), vec)
    vec = jnp.where(lane // 64 == x % 2, vec, 0.0).astype(BF16)
    for p in range(DEVICES):
        pay[p, 64 : 64 + EXTRA, :] = vec
    for group in range(slots // 4):
        for k in range(4 * group, 4 * group + 4):
            for copy in copies[k]:
                copy.wait()
        for r in range(8):
            rows = slice(16 * r, 16 * r + 16)
            tiles = []
            for k in range(4 * group, 4 * group + 4):
                acc = 0.95 * eb[k, rows, :] + (gb[k, rows, :] - lb[k, rows, :].astype(F32))
                tiles.append(jnp.where(k < counts[0, 0, 0], acc, 0.0))
            for q in range(4):
                tile = jnp.concatenate([t[4 * q : 4 * q + 4] for t in tiles], axis=0)
                pay[8 * q + r, 16 * group : 16 * group + 16, :] = tile.astype(BF16)
    held.wait()
    for d, out in enumerate((m0, m1, m2, m3)):
        out[...] = pick((y + d) % 4, [mb[4 * q : 4 * q + 4, :] for q in range(4)])


def tiles_of(flat, tall):
    out = []
    if flat is not None:
        cols = flat.shape[1] * 4 // 5
        for t in range(0, cols // 4, BLOCK):
            out.append((None, slice(cols + t, cols + t + BLOCK), [i * cols // 4 + t for i in range(4)]))
    if tall is not None:
        wide = tall.shape[1]
        for k in range(4):
            for t in range(0, wide, BLOCK):
                out.append((slice(16 * k, 16 * k + 16), slice(t, t + BLOCK), [(4 * k + i) * wide + t for i in range(4)]))
    return out


def share_kernel(recv, base, m0, m1, m2, m3, c1, c2, c3, t1, t2, t3, n0, mb, nb):
    y, _, _ = place()
    for d, m in enumerate((m0, m1, m2, m3)):
        mb[d] = m[...]
    row = lax.broadcasted_iota(jnp.int32, (512, BLOCK), 0)
    lane = lax.broadcasted_iota(jnp.int32, (512, BLOCK), 1)
    want = (row // 4 % 4 * 32 + row // 16) * 4 + row % 4
    want = (want - lane % 4).astype(F32)
    total = jnp.zeros((512, BLOCK), F32)
    for i in range(0, DEVICES, 4):
        halves = []
        for h in (i, i + 2):
            pair = recv[h, 64 : 64 + EXTRA, :].astype(F32) + recv[h + 1, 64 : 64 + EXTRA, :].astype(F32)
            halves.append((want == 4.0 * pair[0:1, :]).astype(F32).astype(BF16))
        table = jnp.concatenate(halves, axis=1)
        values = jnp.concatenate([recv[i + s, 0:64, :] for s in range(4)], axis=0)
        total = total + jnp.dot(table, values, preferred_element_type=F32)
    for b in range(32):
        cols = slice(BLOCK * b, BLOCK * b + BLOCK)
        average = total[16 * b : 16 * b + 16, :] * (1.0 / DEVICES)
        mom = jnp.concatenate([mb[(y - q) % 4, :, cols] for q in range(4)], axis=0)
        new_mom = 0.9 * mom + average
        code = encode(base[:, cols] - 0.7 * (average + 0.9 * new_mom))
        for out in (c1, c2, c3):
            out[:, cols] = code
        for q in range(4):
            nb[q, :, cols] = new_mom[4 * q : 4 * q + 4, :]
    n0[...] = nb[y]
    for d, (flat, tall) in enumerate(((c1, t1), (c2, t2), (c3, t3)), 1):
        for rows, cols, places in tiles_of(flat, tall):
            tile = encode(jnp.concatenate([nb[(y + d) % 4, :, p : p + BLOCK] for p in places], axis=0))
            (flat if rows is None else tall)[slice(None) if rows is None else rows, cols] = tile


def group_kernel(c1, r1, r2, r3, t1, t2, t3, g1, g2, g3):
    width = g1.shape[1] - t1.shape[1]
    for n, code in enumerate((c1, r1, r2, r3)):
        part = code[:, :width]
        for out in (g1, g2, g3):
            out[16 * n : 16 * n + 16, :width] = part
    for out, tail in ((g1, t1), (g2, t2), (g3, t3)):
        out[:, width:] = tail[...]


def error_kernel(top, kept, counts, g, l, e, *refs):
    gb, lb, eb, mask, sems, done, rb, rsems = refs[-8:]
    out, base = refs[:2] if top == 0 else (refs[1], None)
    chunks, high, _ = gb.shape
    copies = []
    for i in range(chunks):
        rows = pl.ds(top + i * high, high)
        copies.append([
            pltpu.make_async_copy(src.at[rows, :], dst.at[i], sems.at[n, i])
            for n, (src, dst) in enumerate(((g, gb), (l, lb), (e, eb)))
        ])
        for copy in copies[-1]:
            copy.start()
    if base is not None:
        y, c, x = place()
        reads = []
        for q in range(4):
            rows = pl.ds(pl.multiple_of(q * BLOCK + 16 * (4 * c + x), 16), 16)
            reads.append(pltpu.make_async_copy(g.at[rows, :], rb.at[q], rsems.at[q]))
            reads[-1].start()
    for n in range(mask.shape[0]):
        mask[n] = jnp.int32(0)
    for k in range(kept.shape[-1]):

        @pl.when(k < counts[0, 0, 0])
        def _():
            mask[kept[0, 0, 0, k]] = jnp.int32(1)

    back = []
    for i in range(chunks):
        for copy in copies[i]:
            copy.wait()
        first = (top + i * high) // BLOCK * 32

        def body(b, _):
            cols = pl.ds(pl.multiple_of(b * BLOCK, BLOCK), BLOCK)
            acc = 0.95 * eb[i, :, cols] + (gb[i, :, cols] - lb[i, :, cols].astype(F32))
            kept = mask[first + b] > 0
            eb[i, :, cols] = acc - jnp.where(kept, acc.astype(BF16).astype(F32), 0.0)
            return 0

        lax.fori_loop(0, 32, body, 0, unroll=4)
        back.append(pltpu.make_async_copy(eb.at[i], out.at[pl.ds(top + i * high, high), :], done.at[i]))
        back[-1].start()
    if base is not None:
        for q in range(4):
            reads[q].wait()
            base[4 * q : 4 * q + 4, :] = pick(y, [rb[q, 4 * n : 4 * n + 4, :] for n in range(4)])
    for copy in back:
        copy.wait()


def spread_kernel(mine, *refs):
    groups, (stage, sems) = refs[:4], refs[-2:]
    out = refs[8] if mine else refs[5]
    y, c, x = place()
    half = c if mine else 1 - c
    width = BLOCK

    def unit(slot, tile, parts_of):
        def body(i, _):
            cols = pl.ds(pl.multiple_of(i * width, width), width)
            parts = [decode(part) for part in parts_of(cols)]
            for q in range(4):
                stage[slot, q, :, cols] = jnp.concatenate([p[4 * q : 4 * q + 4, :] for p in parts], axis=0)
            return 0

        rows = pl.ds(pl.multiple_of(tile * 16, 16), 16)
        part = stage.shape[3] // PIECES
        for n in range(PIECES):
            lax.fori_loop(n * part // width, (n + 1) * part // width, body, 0, unroll=True)
            cols = pl.ds(n * part, part)
            pltpu.make_async_copy(stage.at[slot, :, :, cols], out.at[:, rows, cols], sems.at[slot]).start()

    def shard(ref, index, cols):
        return ref[pl.ds(pl.multiple_of(index * 16, 16), 16), cols]

    @pl.when(half == 1)
    def _():
        for d in range(4):
            unit(d, 4 + (x - d) % 4, lambda cols: [shard(groups[d], (y - q) % 4, cols) for q in range(4)])

    for row in range(4):

        @pl.when((half == 0) & (y == row))
        def _():
            def each(d, _):
                unit(d, (x - d) % 4, lambda cols: [shard(groups[(row - q) % 4], d, cols) for q in range(4)])
                return 0

            lax.fori_loop(0, 4, each, 0)

    if mine:
        flats, n0, new_mom, nb = refs[4:7], refs[7], refs[9], refs[10]
        nb[y] = n0[...]
        full = nb.shape[2]

        def place_piece(d, ref, first, flat, tall):
            for rows, cols, places in tiles_of(flat, tall):
                cols = slice(cols.start + first, cols.stop + first)
                tile = decode(ref[slice(None) if rows is None else rows, cols])
                for n, p in enumerate(places):
                    nb[(y - d) % 4, :, p : p + BLOCK] = tile[4 * n : 4 * n + 4, :]

        @pl.when(c == 1)
        def _():
            for d, flat in enumerate(flats, 1):
                place_piece(d, flat, 0, flat, None)

        @pl.when(c == 0)
        def _():
            for d, group in enumerate(groups[1:], 1):
                place_piece(d, group, full, None, jax.ShapeDtypeStruct((64, full // 16), BF16))

        for q in range(4):
            new_mom[4 * q : 4 * q + 4, :] = nb[q]
    for slot in range(4):
        pltpu.make_async_copy(stage.at[slot], out.at[:, pl.ds(0, 16), :], sems.at[slot]).wait()


def smem():
    return pl.BlockSpec(memory_space=pltpu.SMEM)


def vmem():
    return pl.BlockSpec(memory_space=pltpu.VMEM)


def hbm():
    return pl.BlockSpec(memory_space=pl.ANY)


def params(mib):
    return pltpu.CompilerParams(vmem_limit_bytes=mib * MIB)


def in_hbm(array):
    return pltpu.with_memory_space_constraint(array, pltpu.HBM)


def error_rows(top, count_rows, high, kept, counts, g, l, e, before):
    rows, cols = g.shape
    chunks = count_rows // high
    given = [] if before is None else [before]
    return pl.pallas_call(
        functools.partial(error_kernel, top),
        out_shape=[jax.ShapeDtypeStruct((rows, cols), F32)] + [jax.ShapeDtypeStruct((16, cols), F32)] * (1 - len(given)),
        in_specs=[smem(), smem()] + [hbm()] * (3 + len(given)),
        out_specs=[hbm()] + [vmem()] * (1 - len(given)),
        input_output_aliases={5: 0} if given else {},
        scratch_shapes=[
            pltpu.VMEM((chunks, high, cols), F32),
            pltpu.VMEM((chunks, high, cols), BF16),
            pltpu.VMEM((chunks, high, cols), F32),
            pltpu.SMEM((rows // BLOCK * (cols // BLOCK),), jnp.int32),
            pltpu.SemaphoreType.DMA((3, chunks)),
            pltpu.SemaphoreType.DMA((chunks,)),
            pltpu.VMEM((4, 16, cols), F32),
            pltpu.SemaphoreType.DMA((4,)),
        ],
        compiler_params=params(4 + 10 * count_rows * cols // MIB),
        cost_estimate=pl.CostEstimate(flops=16 * count_rows * cols, bytes_accessed=14 * count_rows * cols, transcendentals=0),
        name=f"error{top}",
    )(kept, counts, in_hbm(g), in_hbm(l), in_hbm(e), *given)


def spread(groups, cols, before=None, rest=()):
    sds = jax.ShapeDtypeStruct
    mine = before is None
    return pl.pallas_call(
        functools.partial(spread_kernel, mine),
        out_shape=[sds((4, BLOCK, cols), F32)] + [sds((16, cols), F32)] * mine,
        in_specs=[vmem()] * (4 + len(rest)) + [hbm()] * (1 - mine),
        out_specs=[hbm()] + [vmem()] * mine,
        input_output_aliases={} if mine else {4: 0},
        scratch_shapes=[pltpu.VMEM((4, 4, cols), F32)] * mine
        + [pltpu.VMEM((4, 4, 16, cols), F32), pltpu.SemaphoreType.DMA((4,))],
        compiler_params=params(16),
        cost_estimate=pl.CostEstimate(flops=8 * MIB, bytes_accessed=6 * MIB, transcendentals=2 * MIB),
        name="spread_mine" if mine else "spread_other",
    )(*groups, *rest, *([] if mine else [before]))


CUTS = (0, 256, 320, 448, 512)
HIGH = 64
PIECES = 4


def per_device(global_params, local_params, error_buf, momentum, kept, counts):
    rows, cols = global_params.shape
    local, error = local_params.reshape(rows, cols), error_buf.reshape(rows, cols)
    slots = kept.shape[-1]
    sds = jax.ShapeDtypeStruct

    quarter = sds((4, cols), F32)
    pay, m0, m1, m2, m3 = pl.pallas_call(
        pack_kernel,
        out_shape=(pltpu.VMEM((DEVICES, 64 + EXTRA, BLOCK), BF16),) + (quarter,) * 4,
        in_specs=[smem(), smem(), hbm(), hbm(), hbm(), hbm()],
        out_specs=(vmem(),) * 5,
        scratch_shapes=[
            pltpu.VMEM((slots, BLOCK, BLOCK), F32),
            pltpu.VMEM((slots, BLOCK, BLOCK), BF16),
            pltpu.VMEM((slots, BLOCK, BLOCK), F32),
            pltpu.VMEM(momentum.shape, F32),
            pltpu.SemaphoreType.DMA((3, slots)),
            pltpu.SemaphoreType.DMA,
        ],
        compiler_params=params(16),
        cost_estimate=pl.CostEstimate(flops=2 * MIB, bytes_accessed=4 * MIB, transcendentals=0),
        name="pack",
    )(kept, counts, in_hbm(global_params), in_hbm(local), in_hbm(error), in_hbm(momentum))

    m2, m1, m3 = [move(m, lambda y, c, x, d=d: (y + d, c, x)) for d, m in ((2, m2), (1, m1), (3, m3))]
    recv = lax.all_to_all(pay, AXES, 0, 0, tiled=True)
    def part(n, local, before):
        return error_rows(CUTS[n], CUTS[n + 1] - CUTS[n], HIGH, kept, counts, global_params, local, error, before)

    pay, local = lax.optimization_barrier((pay, local))
    new_error, base = part(0, local, None)
    recv, new_error, base = lax.optimization_barrier((recv, new_error, base))

    flat, tall = sds((16, cols + cols // 4), BF16), sds((64, cols // 16), BF16)
    *codes, t1, t2, t3, n0 = pl.pallas_call(
        share_kernel,
        out_shape=(flat,) * 3 + (tall,) * 3 + (quarter,),
        in_specs=[vmem()] * 6,
        out_specs=(vmem(),) * 7,
        scratch_shapes=[pltpu.VMEM((4, 4, cols), F32)] * 2,
        compiler_params=params(16),
        cost_estimate=pl.CostEstimate(flops=256 * MIB, bytes_accessed=4 * MIB, transcendentals=0),
        name="share",
    )(recv, base, m0, m1, m2, m3)

    codes[0], local = lax.optimization_barrier((codes[0], local))
    new_error, = part(1, local, new_error)
    first = [
        move(code, lambda y, c, x, d=d: (y, c, x + d) if c == 0 else (y + d, c, x)) for d, code in enumerate(codes, 1)
    ]
    first, new_error = lax.optimization_barrier((first, new_error))
    g1, g2, g3 = pl.pallas_call(
        group_kernel,
        out_shape=(sds((64, cols + cols // 16), BF16),) * 3,
        in_specs=[vmem()] * 7,
        out_specs=(vmem(),) * 3,
        compiler_params=params(16),
        cost_estimate=pl.CostEstimate(flops=0, bytes_accessed=2 * MIB, transcendentals=0),
        name="group",
    )(codes[0], *first, t1, t2, t3)

    def send(group, d):
        return move(group, lambda y, c, x: (y + d, c, x) if c == 0 else (y, c, x + d))

    def swap(group):
        return move(group, lambda y, c, x: (y, c + 1, x))

    g1, g2, g3, local = lax.optimization_barrier((g1, g2, g3, local))
    own = [g1] + [send(g, d) for d, g in enumerate((g1, g2, g3), 1)]
    new_error, = part(2, local, new_error)
    own[2], local, new_error = lax.optimization_barrier((own[2], local, new_error))
    other0, other2 = swap(own[0]), swap(own[2])
    new_error, = part(3, local, new_error)
    own[1], own[3], other0, other2, new_error = lax.optimization_barrier((own[1], own[3], other0, other2, new_error))
    other = [other0, swap(own[1]), other2, swap(own[3])]
    new_params, new_mom = spread(own, cols, None, [*first, n0])
    new_params, = spread(other, cols, new_params)
    return (
        new_params.reshape(rows, cols),
        new_error.reshape(1, 1, rows, cols),
        new_mom,
    )


def solution(mesh):
    return jax.shard_map(
        per_device,
        mesh=mesh,
        in_specs=(
            P(None, "tensor"),
            P("region", "island", None, "tensor"),
            P("region", "island", None, "tensor"),
            P(("island", "region"), "tensor"),
            P("region", "island", "tensor", None),
            P("region", "island", "tensor"),
        ),
        out_specs=(
            P(None, "tensor"),
            P("region", "island", None, "tensor"),
            P(("island", "region"), "tensor"),
        ),
        check_vma=False,
    )
```
